256 devices in a mesh: seq: 32 (over x, y, core), kvh: 8 (over z).
Axes of the slice: x: 4, y: 4, z: 8, core: 2. Of those that a mesh axis runs over, the one named last changes fastest.
Arguments:
- queries: bfloat16 [512, 64, 128], P(('seq', 'kvh')), may hold values from -9 to 9
- attn_out: bfloat16 [512, 64, 128], P(('seq', 'kvh')), may hold values from -0.59765625 to 0.59765625
- grad_out: bfloat16 [512, 64, 128], P(('seq', 'kvh')), may hold values from -384 to 384
- log_norms: float32 [512, 64], P(('seq', 'kvh')), may hold values from 0 to 14, as said below
- query_starts: int32 [512], replicated, may hold values from 0 to 8192
- keys: bfloat16 [32768, 8, 128], P('seq', 'kvh'), may hold values from -6 to 6
- values: bfloat16 [32768, 8, 128], P('seq', 'kvh'), may hold values from -6 to 6
Outputs:
- grad_query: bfloat16 [512, 64, 128], P(('seq', 'kvh'))
- grad_keys: bfloat16 [32768, 8, 128], P('seq', 'kvh')
- grad_values: bfloat16 [32768, 8, 128], P('seq', 'kvh')
The draws below stay inside these ranges and needn't reach their ends.
Inputs may be any that keep to these rules, and one draw needn't show every extreme that they name: `log_norms`: each entry lies within one of the log of its token's number of visible positions plus 1.125.
All inputs are finite; a program needn't handle non-finite values.
Results may differ from the reference program's by a relative error of at most 0.0052.
Values may be sent and summed in bfloat16 or wider, within the bound.
A program may use at most 64 MiB of HBM per device.

```python
import jax
import jax.numpy as jnp
from jax import lax

HD = 128
GROUP = 8
KEY_DEV = 1024
KVH = 8
H = 64
CTX = 32768
Q_TOK = 512
N_SEQ = 32


def first_positions(key):
    highest = CTX // 4
    starts = jax.random.randint(jax.random.fold_in(key, 5), (Q_TOK,), 0, highest + 1, dtype=jnp.int32)
    order = jax.random.permutation(jax.random.fold_in(key, 7), Q_TOK)
    places = jnp.arange(Q_TOK, dtype=jnp.int32)
    starts = jnp.where(places == order[0], 0, starts)
    starts = jnp.where(places == order[1], highest, starts)
    return starts.astype(jnp.int32)


def draw_query_starts(key, part):
    return first_positions(key)


def draw_log_norms(key, part):
    firsts = first_positions(key)
    position = CTX - Q_TOK + jnp.arange(Q_TOK, dtype=jnp.int32)
    counts = (position - firsts + 1).astype(jnp.float32)
    baseline = jnp.log(counts) + 1.125
    jitter = jnp.clip(0.3 * jax.random.normal(jax.random.fold_in(key, 11), (Q_TOK, H), jnp.float32), -1.0, 1.0)
    return baseline[:, None] + jitter


def shard_levels(stream_key, shape, shards, smallest, high):
    loudness, own = 1.0, jax.random.fold_in(stream_key, 6)
    for axis_at, parts in shards:
        heights = jnp.exp(jax.random.uniform(jax.random.fold_in(own, axis_at), (parts,), jnp.float32, smallest / len(shards), high / len(shards)))
        loudness = loudness * jnp.repeat(heights, shape[axis_at] // parts).reshape([-1 if axis == axis_at else 1 for axis in range(len(shape))])
    return loudness


def gaussian(own_key, extent, spread, bound, split=(), kind=jnp.bfloat16):
    array = spread * jax.random.normal(own_key, extent, jnp.float32)
    if split:
        array = array * shard_levels(own_key, extent, split, -0.22, 0.18)
    return jnp.clip(array, -bound, bound).astype(kind)


def setup_inputs(seed: int = 0) -> dict:
    key_of = jax.random.split(jax.random.key(seed), 8)
    queries = gaussian(key_of[0], (Q_TOK, H, HD), 1.5, 9.0, ((0, 256),))
    attn_out = gaussian(key_of[1], (Q_TOK, H, HD), 0.1, 0.59765625, ((0, 256),))
    grad_out = gaussian(key_of[2], (Q_TOK, H, HD), 64.0, 384.0, ((0, 256),))
    log_norms = draw_log_norms(jax.random.fold_in(key_of[7], 71), 0)
    query_starts = draw_query_starts(jax.random.fold_in(key_of[7], 71), 0)
    keys = gaussian(key_of[5], (CTX, KVH, HD), 1.0, 6.0, ((0, 32), (1, 8)))
    values = gaussian(key_of[6], (CTX, KVH, HD), 1.0, 6.0, ((0, 32), (1, 8)))
    return {"queries": queries, "attn_out": attn_out, "grad_out": grad_out, "log_norms": log_norms, "query_starts": query_starts, "keys": keys, "values": values}


def reference(queries, attn_out, grad_out, log_norms, query_starts, keys, values):
    scaling = HD ** -0.5
    deltas = jnp.sum(grad_out.astype(jnp.float32) * attn_out.astype(jnp.float32), axis=-1)
    query_wide = queries.astype(jnp.float32).reshape(Q_TOK, KVH, GROUP, HD)
    grad_wide = grad_out.astype(jnp.float32).reshape(Q_TOK, KVH, GROUP, HD)
    norm_grid = log_norms.reshape(Q_TOK, KVH, GROUP)
    delta_grid = deltas.reshape(Q_TOK, KVH, GROUP)
    query_pos = CTX - Q_TOK + jnp.arange(Q_TOK, dtype=jnp.int32)
    key_blocks = keys.reshape(N_SEQ, KEY_DEV, KVH, HD)
    value_blocks = values.reshape(N_SEQ, KEY_DEV, KVH, HD)

    def visit_owner(grad_query, inputs):
        block_index, key_block, value_block = inputs
        key_pos = block_index * KEY_DEV + jnp.arange(KEY_DEV, dtype=jnp.int32)
        visible = (key_pos[None, :] >= query_starts[:, None]) & (key_pos[None, :] <= query_pos[:, None])
        key_wide = key_block.astype(jnp.float32)
        value_wide = value_block.astype(jnp.float32)
        scores = jnp.einsum("qngd,knd->qngk", query_wide, key_wide) * scaling
        weights = jnp.where(visible[:, None, None, :], jnp.exp(scores - norm_grid[..., None]), 0.0)
        weight_grad = jnp.einsum("qngd,knd->qngk", grad_wide, value_wide)
        score_grad = weights * (weight_grad - delta_grid[..., None])
        weight_half = lax.optimization_barrier(weights.astype(jnp.bfloat16)).astype(jnp.float32)
        score_half = lax.optimization_barrier(score_grad.astype(jnp.bfloat16)).astype(jnp.float32)
        value_grad = jnp.einsum("qngk,qngd->knd", weight_half, grad_wide)
        key_grad = jnp.einsum("qngk,qngd->knd", score_half, query_wide) * scaling
        grad_query = grad_query + jnp.einsum("qngk,knd->qngd", score_half, key_wide) * scaling
        return grad_query, (key_grad.astype(jnp.bfloat16), value_grad.astype(jnp.bfloat16))

    initial = jnp.zeros((Q_TOK, KVH, GROUP, HD), jnp.float32)
    indices = jnp.arange(N_SEQ, dtype=jnp.int32)
    grad_query, (key_grads, value_grads) = lax.scan(visit_owner, initial, (indices, key_blocks, value_blocks))
    return (grad_query.reshape(Q_TOK, H, HD).astype(jnp.bfloat16),
            key_grads.reshape(CTX, KVH, HD),
            value_grads.reshape(CTX, KVH, HD))
```

```python
import functools
import math

import jax
import jax.numpy as jnp
from jax import lax
from jax.experimental import pallas as pl
from jax.experimental.pallas import tpu as pltpu
from jax.sharding import PartitionSpec as P

F32, BF16 = jnp.float32, jnp.bfloat16
MESH = pl.DeviceIdType.MESH

ROWS = 128
BLOCK = 2 * ROWS + 16
HALVES = {"all": (0, BLOCK), "a": (0, ROWS), "b": (ROWS, BLOCK - ROWS)}

CHUNKS = (
    (("o", (0, 0)), ("s", (0, 0))),
    (("o", (1, 0)), ("o", (3, 0))),
    (("s", (1, 0)), ("s", (3, 0))),
    (("o", (0, 1)), ("s", (0, 1))),
    (("o", (2, 0)), ("s", (2, 0))),
    (("o", (1, 1)), ("o", (1, 3))),
    (("o", (3, 1)), ("o", (3, 3))),
    (("s", (1, 1)), ("s", (1, 3))),
    (("s", (3, 1)), ("s", (3, 3))),
    (("o", (2, 1)), ("o", (2, 3))),
    (("s", (2, 1)), ("s", (2, 3))),
    (("o", (0, 2)), ("s", (0, 2))),
    (("o", (1, 2)), ("o", (3, 2))),
    (("s", (1, 2)), ("s", (3, 2))),
    (("o", (2, 2)), ("s", (2, 2))),
    (("o", (0, 3)), ("s", (0, 3))),
)
ARRIVE = {
    1: ((1, 0), (3, 0)),
    2: ((0, 1), (0, 3)),
    3: ((2, 0),),
    4: ((1, 1), (1, 3)),
    5: ((3, 1), (3, 3)),
    6: ((0, 2),),
    7: ((2, 1), (2, 3)),
    8: ((1, 2),),
    9: ((3, 2),),
    10: ((2, 2),),
}
SLOT = {name: 2 * c + i for c, pair in enumerate(CHUNKS) for i, name in enumerate(pair)}
CHUNK_OF = {name: c for c, pair in enumerate(CHUNKS) for name in pair}
PLACES = [(a, b) for a in range(4) for b in range(4)]
NUMBER = {place: i for i, place in enumerate(PLACES)}
MOVES = [((0, 0), (1, 0), "all", "p+"), ((0, 0), (3, 0), "all", "p-")]
MOVES += [((0, 0), (0, 1), "all", "q+"), ((0, 0), (0, 3), "all", "q-")]
MOVES += [((1, 0), (2, 0), "a", "p+"), ((3, 0), (2, 0), "b", "p-")]
for _a in (1, 3, 2):
    MOVES += [((_a, 0), (_a, 1), "all", "q+"), ((_a, 0), (_a, 3), "all", "q-")]
for _a in (0, 1, 3, 2):
    MOVES += [((_a, 1), (_a, 2), "a", "q+"), ((_a, 3), (_a, 2), "b", "q-")]
MOVES += [(place, place, "all", "sib") for place in PLACES]


def kernel(
    scaling,
    q_hbm, o_hbm, g_hbm, n_hbm, st_hbm, k_hbm, v_hbm,
    dq_ref, dk_hbm, dv_hbm,
    q_in, o_in, g_in, n_in, st_in, keys, vals, keys_t, jpos,
    stage, landed, blocks, part, part_half, part_in, total_half, total_in,
    dk_acc, dv_acc, dk_half, dv_half, fin, fin_in,
    in_sem, az_send, az_recv, mv_send, mv_recv, ps_send, ps_recv, tt_send, tt_recv,
    fz_send, fz_recv,
):
    s, k = lax.axis_index("seq"), lax.axis_index("kvh")
    x, y, core = s // 8, (s // 2) % 4, s % 2
    pa, pb = (1 - core) * x + core * y, (1 - core) * y + core * x

    def at(a, b):
        return (1 - core) * ((a * 4 + b) * 2) + core * ((b * 4 + a) * 2 + 1)

    sibling = s + 1 - 2 * core
    target = {
        "p+": at((pa + 1) % 4, pb),
        "p-": at((pa + 3) % 4, pb),
        "q+": at(pa, (pb + 1) % 4),
        "q-": at(pa, (pb + 3) % 4),
        "sib": sibling,
    }

    ins = [
        pltpu.make_async_copy(src, dst, in_sem.at[i])
        for i, (src, dst) in enumerate(
            (
                (g_hbm, g_in), (o_hbm, o_in), (n_hbm, n_in), (st_hbm, st_in), (q_hbm, q_in),
                (k_hbm, keys), (v_hbm, vals),
            )
        )
    ]
    for copy in ins:
        copy.start()

    barrier = pltpu.get_barrier_semaphore()
    for j in range(1, 8):
        pl.semaphore_signal(
            barrier, inc=1, device_id={"kvh": (k + j) % 8}, device_id_type=MESH
        )
    for a, b in PLACES[1:]:
        pl.semaphore_signal(
            barrier, inc=1, device_id={"seq": at((pa + a) % 4, (pb + b) % 4)}, device_id_type=MESH
        )
    pl.semaphore_signal(barrier, inc=1, device_id={"seq": sibling}, device_id_type=MESH)

    def move(n):
        source, dest, half, way = MOVES[n]
        first, count = HALVES[half]
        kind = "s" if way == "sib" else "o"
        return pltpu.make_async_remote_copy(
            src_ref=blocks.at[SLOT["o", source], pl.ds(first, count)],
            dst_ref=blocks.at[SLOT[kind, dest], pl.ds(first, count)],
            send_sem=mv_send.at[n],
            recv_sem=mv_recv.at[n],
            device_id={"seq": target[way]},
            device_id_type=MESH,
        )

    def pass_on(place):
        for n, m in enumerate(MOVES):
            if m[0] == place:
                move(n).start()

    def arrived(kind, place):
        for n, m in enumerate(MOVES):
            if m[1] == place and (m[3] == "sib") == (kind == "s"):
                move(n).wait_recv()

    def give_part(place):
        n = NUMBER[place]
        return pltpu.make_async_remote_copy(
            src_ref=part_half.at[SLOT["s", place]],
            dst_ref=part_in.at[n],
            send_sem=ps_send.at[n],
            recv_sem=ps_recv.at[n],
            device_id={"seq": sibling},
            device_id_type=MESH,
        )

    def give_total(place):
        n = NUMBER[place]
        a, b = place
        return pltpu.make_async_remote_copy(
            src_ref=total_half.at[n],
            dst_ref=total_in.at[n],
            send_sem=tt_send.at[n],
            recv_sem=tt_recv.at[n],
            device_id={"seq": at((pa - a + 4) % 4, (pb - b + 4) % 4)},
            device_id_type=MESH,
        )

    def combine(place):
        give_part(place).wait_recv()
        n = NUMBER[place]
        both = part[SLOT["o", place]] + part_in[n].astype(F32)
        if place == (0, 0):
            part[SLOT["o", place]] = both
        else:
            total_half[n] = both.astype(BF16)
            give_total(place).start()

    for copy in ins[:5]:
        copy.wait()
    heads = 8
    grads = g_in[...].astype(F32)
    queries = q_in[...].astype(F32)
    for j in range(8):
        rows = slice(heads * j, heads * (j + 1))
        stage[j, 0:16] = jnp.concatenate([queries[0, rows], queries[1, rows]], axis=0).astype(BF16)
        stage[j, 16:32] = jnp.concatenate([grads[0, rows], grads[1, rows]], axis=0).astype(BF16)
    product = (grads * o_in[...].astype(F32)).reshape(ROWS, 128)
    product_hi = product.astype(BF16)
    product_lo = (product - product_hi.astype(F32)).astype(BF16)
    ones = jnp.ones((16, 128), BF16)
    contract_last = (((1,), (1,)), ((), ()))
    delta = lax.dot_general(ones, product_hi, contract_last, preferred_element_type=F32)
    delta = delta + lax.dot_general(ones, product_lo, contract_last, preferred_element_type=F32)
    norm = n_in[...] * math.log2(math.e)
    norm = jnp.broadcast_to(
        jnp.concatenate([norm[0:1], norm[1:2]], axis=1), (16, 128)
    )

    row = lax.broadcasted_iota(jnp.int32, (16, 128), 0)
    lane = lax.broadcasted_iota(jnp.int32, (16, 128), 1)
    token = 16 * s + 2 * k
    start = jnp.where(lane < 64, st_in[token], st_in[token + 1])

    def parts_of(value):
        hi = value.astype(BF16).astype(F32)
        mid = (value - hi).astype(BF16).astype(F32)
        return hi, mid, value - hi - mid

    numbers = (
        *parts_of(norm),
        *parts_of(delta),
        (start // 128).astype(F32),
        (start % 128).astype(F32),
        jnp.full((16, 128), s, jnp.int32).astype(F32),
    )
    base = jnp.zeros((16, 128), F32)
    for i, value in enumerate(numbers):
        base = jnp.where(row == i, value, base)
    big_row = lax.broadcasted_iota(jnp.int32, (128, 128), 0)
    big_lane = lax.broadcasted_iota(jnp.int32, (128, 128), 1)
    spread = jnp.concatenate([base] * 8, axis=0)
    spread = jnp.where((big_lane % 64) // 8 == big_row // 16, spread, 0.0).astype(BF16)
    places = 16 * k + 8 * (big_row // 64) + big_row % 8
    pick = jnp.where(big_lane == places, 1.0, 0.0).astype(BF16)
    spread = jnp.dot(spread, pick, preferred_element_type=F32).astype(BF16)
    for j in range(8):
        stage[j, 32:48] = spread[16 * j : 16 * (j + 1)]

    pl.semaphore_wait(barrier, 7 + 15 + 1)

    def hand_out(j):
        peer = (k + j) % 8
        return pltpu.make_async_remote_copy(
            src_ref=stage.at[peer],
            dst_ref=landed.at[k],
            send_sem=az_send.at[j],
            recv_sem=az_recv.at[j],
            device_id={"kvh": peer},
            device_id_type=MESH,
        )

    def hand_in(j):
        return pltpu.make_async_remote_copy(
            src_ref=stage.at[(k + j) % 8],
            dst_ref=landed.at[(k + 8 - j) % 8],
            send_sem=az_send.at[j],
            recv_sem=az_recv.at[j],
            device_id={"kvh": (k + j) % 8},
            device_id_type=MESH,
        )

    for j in (4, 3, 5, 2, 6, 1, 7):
        hand_out(j).start()
    landed[k] = stage[k]
    key_count = keys.shape[0]
    for copy in ins[5:]:
        copy.wait()
    keys_t[...] = keys[...].astype(F32).T.astype(BF16)
    is_last = jnp.where(s == 31, 1.0, 0.0).astype(F32)
    sign = 1.0 - 2.0 * is_last
    jpos[...] = sign * lax.broadcasted_iota(jnp.int32, (key_count, 128), 0).astype(F32)
    dk_acc[...] = jnp.zeros_like(dk_acc)
    dv_acc[...] = jnp.zeros_like(dv_acc)
    for j in range(1, 8):
        hand_in(j).wait_recv()
    mine = SLOT["o", (0, 0)]
    aux = jnp.zeros((16, 128), F32)
    for j in range(8):
        blocks[mine, 16 * j : 16 * (j + 1)] = landed[j, 0:16]
        blocks[mine, ROWS + 16 * j : ROWS + 16 * (j + 1)] = landed[j, 16:32]
        aux = aux + landed[j, 32:48].astype(F32)
    blocks[mine, 2 * ROWS : BLOCK] = aux.astype(BF16)
    pass_on((0, 0))

    shift = (s * key_count).astype(F32)
    in_block = (lax.broadcasted_iota(jnp.int32, (1, 256), 1) % 128) // 8
    last_bound = -(512.0 + in_block.astype(F32))
    factor = scaling * math.log2(math.e)
    tile = 256

    def chunk_step(c, carry):
        for at_chunk in range(16):
            def events(at_chunk=at_chunk):
                for place in ARRIVE.get(at_chunk, ()):
                    arrived("o", place)
                    pass_on(place)
                for kind, place in CHUNKS[at_chunk]:
                    if kind == "s":
                        arrived("s", place)
                for place in PLACES:
                    if CHUNK_OF["s", place] + 2 == at_chunk:
                        combine(place)

            pl.when(c == at_chunk)(events)

        aux = jnp.concatenate(
            [blocks[2 * c + i, 2 * ROWS : BLOCK].astype(F32) for i in range(2)], axis=1
        )
        norm = aux[0:1] + aux[1:2] + aux[2:3]
        delta = aux[3:4] + aux[4:5] + aux[5:6]
        first = aux[6:7] * 128.0 + aux[7:8] - shift
        bound = jnp.where(is_last > 0.5, last_bound - 16.0 * aux[8:9], first)
        q = blocks[pl.ds(2 * c, 2), 0:ROWS].reshape(2 * ROWS, 128)
        g = blocks[pl.ds(2 * c, 2), ROWS : 2 * ROWS].reshape(2 * ROWS, 128)
        dq = jnp.zeros((128, 2 * ROWS), F32)
        for t in range(key_count // tile):
            here = slice(t * tile, (t + 1) * tile)
            scores = lax.dot_general(keys[here], q, contract_last, preferred_element_type=F32)
            pos = jpos[here]
            pos = jnp.concatenate([pos, pos], axis=1)
            weights = jnp.where(pos >= bound, jnp.exp2(scores * factor - norm), 0.0)
            grads = lax.dot_general(vals[here], g, contract_last, preferred_element_type=F32)
            score_half = (weights * (grads - delta)).astype(BF16)
            dv_acc[here] += jnp.dot(weights.astype(BF16), g, preferred_element_type=F32)
            dk_acc[here] += jnp.dot(score_half, q, preferred_element_type=F32)
            dq = dq + jnp.dot(keys_t[:, here], score_half, preferred_element_type=F32)
        for i in range(2):
            mine = dq[:, i * ROWS : (i + 1) * ROWS]
            part[2 * c + i] = mine
            part_half[2 * c + i] = mine.astype(BF16)

        for at_chunk in range(16):
            def give(at_chunk=at_chunk):
                for kind, place in CHUNKS[at_chunk]:
                    if kind == "s":
                        give_part(place).start()

            if any(kind == "s" for kind, _ in CHUNKS[at_chunk]):
                pl.when(c == at_chunk)(give)
        return carry

    lax.fori_loop(0, 16, chunk_step, 0)

    late = [place for place in PLACES if CHUNK_OF["s", place] + 2 > 15]
    late = sorted(late, key=lambda place: CHUNK_OF["s", place])
    for place in late[:-1]:
        combine(place)
    dk_half[...] = (dk_acc[...] * scaling).astype(BF16)
    out_k = pltpu.make_async_copy(dk_half, dk_hbm, in_sem.at[0])
    out_k.start()
    combine(late[-1])
    dv_half[...] = dv_acc[...].astype(BF16)
    out_v = pltpu.make_async_copy(dv_half, dv_hbm, in_sem.at[1])
    out_v.start()

    total = part[SLOT["o", (0, 0)]]
    for place in PLACES[1:]:
        give_total(place).wait_recv()
        total = total + total_in[NUMBER[place]].astype(F32)
    fin[...] = (total.T * scaling).astype(BF16)

    def send_back(j):
        peer = (k + j) % 8
        return pltpu.make_async_remote_copy(
            src_ref=fin.at[pl.ds(pl.multiple_of(16 * peer, 16), 16)],
            dst_ref=fin_in.at[k],
            send_sem=fz_send.at[j],
            recv_sem=fz_recv.at[j],
            device_id={"kvh": peer},
            device_id_type=MESH,
        )

    def come_back(j):
        peer = (k + j) % 8
        return pltpu.make_async_remote_copy(
            src_ref=fin.at[pl.ds(pl.multiple_of(16 * peer, 16), 16)],
            dst_ref=fin_in.at[(k + 8 - j) % 8],
            send_sem=fz_send.at[j],
            recv_sem=fz_recv.at[j],
            device_id={"kvh": peer},
            device_id_type=MESH,
        )

    for j in (4, 3, 5, 2, 6, 1, 7):
        send_back(j).start()
    fin_in[k] = fin[pl.ds(pl.multiple_of(16 * k, 16), 16)]

    for n in range(len(MOVES)):
        move(n).wait_send()
    for place in PLACES:
        give_part(place).wait_send()
        if place != (0, 0):
            give_total(place).wait_send()
    for j in range(1, 8):
        hand_out(j).wait_send()
    for j in range(1, 8):
        come_back(j).wait_recv()
    both = [fin_in[j].astype(F32) for j in range(8)]
    for t in range(2):
        rows = [b[8 * t : 8 * (t + 1)] for b in both]
        dq_ref[t] = jnp.concatenate(rows, axis=0).astype(BF16)
    for j in range(1, 8):
        send_back(j).wait_send()
    out_k.wait()
    out_v.wait()


def local(queries, attn_out, grad_out, log_norms, query_starts, keys, values):
    scaling = queries.shape[-1] ** (-0.5)
    key_count = keys.shape[0]
    anywhere = pl.BlockSpec(memory_space=pl.ANY)
    sems = [7, 8, 8, len(MOVES), len(MOVES), 16, 16, 16, 16, 8, 8]
    dq, dk, dv = pl.pallas_call(
        functools.partial(kernel, scaling),
        out_shape=(
            jax.ShapeDtypeStruct((2, 64, 128), BF16),
            jax.ShapeDtypeStruct((key_count, 128), BF16),
            jax.ShapeDtypeStruct((key_count, 128), BF16),
        ),
        in_specs=[anywhere] * 7,
        out_specs=(pl.BlockSpec(memory_space=pltpu.VMEM), anywhere, anywhere),
        scratch_shapes=[
            pltpu.VMEM((2, 64, 128), BF16),
            pltpu.VMEM((2, 64, 128), BF16),
            pltpu.VMEM((2, 64, 128), BF16),
            pltpu.VMEM((2, 64), F32),
            pltpu.SMEM((512,), jnp.int32),
            pltpu.VMEM((key_count, 128), BF16),
            pltpu.VMEM((key_count, 128), BF16),
            pltpu.VMEM((128, key_count), BF16),
            pltpu.VMEM((key_count, 128), F32),
            pltpu.VMEM((8, 48, 128), BF16),
            pltpu.VMEM((8, 48, 128), BF16),
            pltpu.VMEM((32, BLOCK, 128), BF16),
            pltpu.VMEM((32, 128, ROWS), F32),
            pltpu.VMEM((32, 128, ROWS), BF16),
            pltpu.VMEM((16, 128, ROWS), BF16),
            pltpu.VMEM((16, 128, ROWS), BF16),
            pltpu.VMEM((16, 128, ROWS), BF16),
            pltpu.VMEM((key_count, 128), F32),
            pltpu.VMEM((key_count, 128), F32),
            pltpu.VMEM((key_count, 128), BF16),
            pltpu.VMEM((key_count, 128), BF16),
            pltpu.VMEM((ROWS, 128), BF16),
            pltpu.VMEM((8, 16, 128), BF16),
            *[pltpu.SemaphoreType.DMA((n,)) for n in sems],
        ],
        cost_estimate=pl.CostEstimate(
            flops=10 * 4096 * key_count * 128,
            bytes_accessed=4 * key_count * 256,
            transcendentals=4096 * key_count,
        ),
        compiler_params=pltpu.CompilerParams(
            collective_id=0, has_side_effects=True, vmem_limit_bytes=40 * 1024 * 1024
        ),
    )(
        queries, attn_out, grad_out, log_norms, query_starts,
        keys.reshape(key_count, 128), values.reshape(key_count, 128),
    )
    return dq, dk[:, None, :], dv[:, None, :]


def solution(mesh):
    return jax.shard_map(
        local,
        mesh=mesh,
        in_specs=(
            P(("seq", "kvh"), None, None),
            P(("seq", "kvh"), None, None),
            P(("seq", "kvh"), None, None),
            P(("seq", "kvh"), None),
            P(),
            P("seq", "kvh", None),
            P("seq", "kvh", None),
        ),
        out_specs=(P(("seq", "kvh"), None, None), P("seq", "kvh", None), P("seq", "kvh", None)),
        check_vma=False,
    )
```

```python
import functools
import math

import jax
import jax.numpy as jnp
from jax import lax
from jax.experimental import pallas as pl
from jax.experimental.pallas import tpu as pltpu
from jax.sharding import PartitionSpec as P

F32, BF16 = jnp.float32, jnp.bfloat16
MESH = pl.DeviceIdType.MESH

ROWS = 128
BLOCK = 2 * ROWS + 16
CHUNKS = (
    (("o", (0, 0)), ("s", (0, 0))),
    (("o", (1, 0)), ("o", (3, 0))),
    (("o", (0, 1)), ("o", (0, 3))),
    (("s", (1, 0)), ("s", (3, 0))),
    (("o", (2, 0)), ("o", (0, 2))),
    (("s", (2, 0)), ("s", (0, 2))),
    (("o", (1, 1)), ("o", (1, 3))),
    (("o", (3, 1)), ("o", (3, 3))),
    (("s", (1, 1)), ("s", (1, 3))),
    (("o", (1, 2)), ("o", (3, 2))),
    (("o", (2, 1)), ("o", (2, 3))),
    (("o", (2, 2)), ("s", (2, 2))),
    (("s", (1, 2)), ("s", (3, 2))),
    (("s", (2, 1)), ("s", (2, 3))),
    (("s", (3, 1)), ("s", (3, 3))),
    (("s", (0, 1)), ("s", (0, 3))),
)
ARRIVE = {
    1: ((1, 0), (3, 0)),
    2: ((2, 0), (0, 1), (0, 3)),
    4: ((0, 2),),
    6: ((1, 1), (1, 3)),
    7: ((3, 1), (3, 3)),
    9: ((1, 2), (3, 2)),
    10: ((2, 1), (2, 3), (2, 2)),
}
LAG = 4
SLOT = {name: 2 * c + i for c, pair in enumerate(CHUNKS) for i, name in enumerate(pair)}
CHUNK_OF = {name: c for c, pair in enumerate(CHUNKS) for name in pair}
PLACES = [(a, b) for a in range(4) for b in range(4)]
NUMBER = {place: i for i, place in enumerate(PLACES)}
MOVES = []
for _d in [(1, 0), (3, 0), (2, 0), (1, 1), (1, 3), (3, 1), (3, 3), (0, 2), (0, 1), (0, 3)]:
    MOVES += [((0, 0), _d, _d)]
for _s, _d in [((1, 0), (1, 2)), ((3, 0), (3, 2)), ((2, 0), (2, 2)), ((2, 0), (2, 1)), ((2, 0), (2, 3))]:
    MOVES += [(_s, _d, (0, _d[1]))]
MOVES = [(place, place, "sib") for place in PLACES] + MOVES


def kernel(
    scaling,
    q_hbm, o_hbm, g_hbm, n_hbm, st_hbm, k_hbm, v_hbm,
    dq_ref, dk_hbm, dv_hbm,
    q_in, o_in, g_in, n_in, st_in, keys, vals, keys_t, jpos,
    stage, landed, blocks, part, part_half, part_in, total_half, total_in,
    score_buf, weight_buf, dk_half, dv_half, fin, fin_in,
    in_sem, az_send, az_recv, mv_send, mv_recv, ps_send, ps_recv, tt_send, tt_recv,
    fz_send, fz_recv,
):
    s, k = lax.axis_index("seq"), lax.axis_index("kvh")
    x, y, core = s // 8, (s // 2) % 4, s % 2
    pa, pb = (1 - core) * x + core * y, (1 - core) * y + core * x

    def at(a, b):
        return (1 - core) * ((a * 4 + b) * 2) + core * ((b * 4 + a) * 2 + 1)

    sibling = s + 1 - 2 * core
    target = {
        "sib": sibling,
    }
    for a, b in PLACES[1:]:
        target[a, b] = at((pa + a) % 4, (pb + b) % 4)

    ins = [
        pltpu.make_async_copy(src, dst, in_sem.at[i])
        for i, (src, dst) in enumerate(
            (
                (g_hbm, g_in), (o_hbm, o_in), (n_hbm, n_in), (st_hbm, st_in), (q_hbm, q_in),
                (k_hbm, keys), (v_hbm, vals),
            )
        )
    ]
    for copy in ins:
        copy.start()

    barrier = pltpu.get_barrier_semaphore()
    for j in range(1, 8):
        pl.semaphore_signal(
            barrier, inc=1, device_id={"kvh": (k + j) % 8}, device_id_type=MESH
        )
    for a, b in PLACES[1:]:
        pl.semaphore_signal(
            barrier, inc=1, device_id={"seq": at((pa + a) % 4, (pb + b) % 4)}, device_id_type=MESH
        )
    pl.semaphore_signal(barrier, inc=1, device_id={"seq": sibling}, device_id_type=MESH)

    def move(n):
        source, dest, way = MOVES[n]
        kind = "s" if way == "sib" else "o"
        return pltpu.make_async_remote_copy(
            src_ref=blocks.at[SLOT["o", source]],
            dst_ref=blocks.at[SLOT[kind, dest]],
            send_sem=mv_send.at[n],
            recv_sem=mv_recv.at[n],
            device_id={"seq": target[way]},
            device_id_type=MESH,
        )

    def pass_on(place):
        for n, m in enumerate(MOVES):
            if m[0] == place:
                move(n).start()

    def arrived(kind, place):
        for n, m in enumerate(MOVES):
            if m[1] == place and (m[2] == "sib") == (kind == "s"):
                move(n).wait_recv()

    def give_part(place):
        n = NUMBER[place]
        return pltpu.make_async_remote_copy(
            src_ref=part_half.at[SLOT["s", place]],
            dst_ref=part_in.at[n],
            send_sem=ps_send.at[n],
            recv_sem=ps_recv.at[n],
            device_id={"seq": sibling},
            device_id_type=MESH,
        )

    def give_total(place):
        n = NUMBER[place]
        a, b = place
        return pltpu.make_async_remote_copy(
            src_ref=total_half.at[n],
            dst_ref=total_in.at[n],
            send_sem=tt_send.at[n],
            recv_sem=tt_recv.at[n],
            device_id={"seq": at((pa - a + 4) % 4, (pb - b + 4) % 4)},
            device_id_type=MESH,
        )

    def combine(place):
        give_part(place).wait_recv()
        n = NUMBER[place]
        both = part[SLOT["o", place]] + part_in[n].astype(F32)
        if place == (0, 0):
            part[SLOT["o", place]] = both
        else:
            total_half[n] = both.astype(BF16)
            give_total(place).start()

    for copy in ins[:5]:
        copy.wait()
    heads = 8
    grads = g_in[...].astype(F32)
    queries = q_in[...].astype(F32)
    for j in range(8):
        rows = slice(heads * j, heads * (j + 1))
        stage[j, 0:16] = jnp.concatenate([queries[0, rows], queries[1, rows]], axis=0).astype(BF16)
        stage[j, 16:32] = jnp.concatenate([grads[0, rows], grads[1, rows]], axis=0).astype(BF16)
    product = (grads * o_in[...].astype(F32)).reshape(ROWS, 128)
    product_hi = product.astype(BF16)
    product_lo = (product - product_hi.astype(F32)).astype(BF16)
    ones = jnp.ones((16, 128), BF16)
    contract_last = (((1,), (1,)), ((), ()))
    delta = lax.dot_general(ones, product_hi, contract_last, preferred_element_type=F32)
    delta = delta + lax.dot_general(ones, product_lo, contract_last, preferred_element_type=F32)
    norm = n_in[...] * math.log2(math.e)
    norm = jnp.broadcast_to(
        jnp.concatenate([norm[0:1], norm[1:2]], axis=1), (16, 128)
    )

    row = lax.broadcasted_iota(jnp.int32, (16, 128), 0)
    lane = lax.broadcasted_iota(jnp.int32, (16, 128), 1)
    token = 16 * s + 2 * k
    start = jnp.where(lane < 64, st_in[token], st_in[token + 1])

    def parts_of(value):
        hi = value.astype(BF16).astype(F32)
        mid = (value - hi).astype(BF16).astype(F32)
        return hi, mid, value - hi - mid

    numbers = (
        *parts_of(norm),
        *parts_of(delta),
        (start // 128).astype(F32),
        (start % 128).astype(F32),
        jnp.full((16, 128), s, jnp.int32).astype(F32),
    )
    base = jnp.zeros((16, 128), F32)
    for i, value in enumerate(numbers):
        base = jnp.where(row == i, value, base)
    big_row = lax.broadcasted_iota(jnp.int32, (128, 128), 0)
    big_lane = lax.broadcasted_iota(jnp.int32, (128, 128), 1)
    spread = jnp.concatenate([base] * 8, axis=0)
    spread = jnp.where((big_lane % 64) // 8 == big_row // 16, spread, 0.0).astype(BF16)
    places = 16 * k + 8 * (big_row // 64) + big_row % 8
    pick = jnp.where(big_lane == places, 1.0, 0.0).astype(BF16)
    spread = jnp.dot(spread, pick, preferred_element_type=F32).astype(BF16)
    for j in range(8):
        stage[j, 32:48] = spread[16 * j : 16 * (j + 1)]

    pl.semaphore_wait(barrier, 7 + 15 + 1)

    def hand_out(j):
        peer = (k + j) % 8
        return pltpu.make_async_remote_copy(
            src_ref=stage.at[peer],
            dst_ref=landed.at[k],
            send_sem=az_send.at[j],
            recv_sem=az_recv.at[j],
            device_id={"kvh": peer},
            device_id_type=MESH,
        )

    def hand_in(j):
        return pltpu.make_async_remote_copy(
            src_ref=stage.at[(k + j) % 8],
            dst_ref=landed.at[(k + 8 - j) % 8],
            send_sem=az_send.at[j],
            recv_sem=az_recv.at[j],
            device_id={"kvh": (k + j) % 8},
            device_id_type=MESH,
        )

    for j in (4, 3, 5, 2, 6, 1, 7):
        hand_out(j).start()
    landed[k] = stage[k]
    key_count = keys.shape[0]
    for copy in ins[5:]:
        copy.wait()
    keys_t[...] = keys[...].astype(F32).T.astype(BF16)
    is_last = jnp.where(s == 31, 1.0, 0.0).astype(F32)
    sign = 1.0 - 2.0 * is_last
    jpos[...] = sign * lax.broadcasted_iota(jnp.int32, (key_count, 128), 0).astype(F32)
    for j in range(1, 8):
        hand_in(j).wait_recv()
    mine = SLOT["o", (0, 0)]
    aux = jnp.zeros((16, 128), F32)
    for j in range(8):
        blocks[mine, 16 * j : 16 * (j + 1)] = landed[j, 0:16]
        blocks[mine, ROWS + 16 * j : ROWS + 16 * (j + 1)] = landed[j, 16:32]
        aux = aux + landed[j, 32:48].astype(F32)
    blocks[mine, 2 * ROWS : BLOCK] = aux.astype(BF16)
    pass_on((0, 0))

    shift = (s * key_count).astype(F32)
    in_block = (lax.broadcasted_iota(jnp.int32, (1, 256), 1) % 128) // 8
    last_bound = -(512.0 + in_block.astype(F32))
    factor = scaling * math.log2(math.e)
    tile = 256

    def rows_of(c, first):
        return blocks[pl.ds(2 * c, 2), first : first + ROWS].reshape(2 * ROWS, 128)

    def query_part(c):
        dq = jnp.dot(keys_t[...], score_buf[c], preferred_element_type=F32)
        for i in range(2):
            mine = dq[:, i * ROWS : (i + 1) * ROWS]
            part[2 * c + i] = mine
            part_half[2 * c + i] = mine.astype(BF16)

    def events(at_chunk):
        for place in ARRIVE.get(at_chunk, ()):
            arrived("o", place)
            pass_on(place)
        for kind, place in CHUNKS[at_chunk]:
            if kind == "s":
                arrived("s", place)
        for place in PLACES:
            if CHUNK_OF["s", place] + LAG == at_chunk:
                combine(place)

    def give(at_chunk):
        if at_chunk:
            for kind, place in CHUNKS[at_chunk - 1]:
                if kind == "s":
                    give_part(place).start()

    def by_chunk(c, low, high, do):
        if high - low == 1:
            do(low)
            return
        middle = (low + high) // 2

        def lower():
            by_chunk(c, low, middle, do)

        def upper():
            by_chunk(c, middle, high, do)

        lax.cond(c < middle, lower, upper)

    def chunk_step(c, carry):
        by_chunk(c, 0, 16, events)

        before = jnp.maximum(c - 1, 0)
        query_part(before)
        aux = jnp.concatenate(
            [blocks[2 * c + i, 2 * ROWS : BLOCK].astype(F32) for i in range(2)], axis=1
        )
        norm = aux[0:1] + aux[1:2] + aux[2:3]
        delta = aux[3:4] + aux[4:5] + aux[5:6]
        first = aux[6:7] * 128.0 + aux[7:8] - shift
        bound = jnp.where(is_last > 0.5, last_bound - 16.0 * aux[8:9], first)
        q, g = rows_of(c, 0), rows_of(c, ROWS)
        for t in range(key_count // tile):
            here = slice(t * tile, (t + 1) * tile)
            scores = lax.dot_general(keys[here], q, contract_last, preferred_element_type=F32)
            pos = jpos[here]
            pos = jnp.concatenate([pos, pos], axis=1)
            weights = jnp.where(pos >= bound, jnp.exp2(scores * factor - norm), 0.0)
            grads = lax.dot_general(vals[here], g, contract_last, preferred_element_type=F32)
            weight_buf[c, here] = weights.astype(BF16)
            score_buf[c, here] = (weights * (grads - delta)).astype(BF16)

        by_chunk(c, 0, 16, give)
        return carry

    score_buf[0] = jnp.zeros(score_buf.shape[1:], BF16)
    lax.fori_loop(0, 16, chunk_step, 0)
    query_part(15)
    for kind, place in CHUNKS[15]:
        if kind == "s":
            give_part(place).start()

    late = [place for place in PLACES if CHUNK_OF["s", place] + LAG > 15]
    late = sorted(late, key=lambda place: CHUNK_OF["s", place])
    final = [place for place in late if CHUNK_OF["s", place] >= 14]
    for place in late:
        if place not in final:
            combine(place)

    def key_tile(t, carry):
        def middle():
            for place in final:
                combine(place)

        pl.when(t == 1)(middle)
        here = pl.ds(pl.multiple_of(t * tile, tile), tile)
        dk = jnp.zeros((tile, 128), F32)
        dv = jnp.zeros((tile, 128), F32)
        for c in range(16):
            dk = dk + jnp.dot(score_buf[c, here], rows_of(c, 0), preferred_element_type=F32)
            dv = dv + jnp.dot(weight_buf[c, here], rows_of(c, ROWS), preferred_element_type=F32)
        dk_half[here] = (dk * scaling).astype(BF16)
        dv_half[here] = dv.astype(BF16)
        return carry

    lax.fori_loop(0, key_count // tile, key_tile, 0)
    out_k = pltpu.make_async_copy(dk_half, dk_hbm, in_sem.at[0])
    out_k.start()
    out_v = pltpu.make_async_copy(dv_half, dv_hbm, in_sem.at[1])
    out_v.start()

    total = part[SLOT["o", (0, 0)]]
    for place in PLACES[1:]:
        give_total(place).wait_recv()
        total = total + total_in[NUMBER[place]].astype(F32)
    fin[...] = (total.T * scaling).astype(BF16)

    def send_back(j):
        peer = (k + j) % 8
        return pltpu.make_async_remote_copy(
            src_ref=fin.at[pl.ds(pl.multiple_of(16 * peer, 16), 16)],
            dst_ref=fin_in.at[k],
            send_sem=fz_send.at[j],
            recv_sem=fz_recv.at[j],
            device_id={"kvh": peer},
            device_id_type=MESH,
        )

    def come_back(j):
        peer = (k + j) % 8
        return pltpu.make_async_remote_copy(
            src_ref=fin.at[pl.ds(pl.multiple_of(16 * peer, 16), 16)],
            dst_ref=fin_in.at[(k + 8 - j) % 8],
            send_sem=fz_send.at[j],
            recv_sem=fz_recv.at[j],
            device_id={"kvh": peer},
            device_id_type=MESH,
        )

    for j in (4, 3, 5, 2, 6, 1, 7):
        send_back(j).start()
    fin_in[k] = fin[pl.ds(pl.multiple_of(16 * k, 16), 16)]

    for n in range(len(MOVES)):
        move(n).wait_send()
    for place in PLACES:
        give_part(place).wait_send()
        if place != (0, 0):
            give_total(place).wait_send()
    for j in range(1, 8):
        hand_out(j).wait_send()
    for j in range(1, 8):
        come_back(j).wait_recv()
    both = [fin_in[j].astype(F32) for j in range(8)]
    for t in range(2):
        rows = [b[8 * t : 8 * (t + 1)] for b in both]
        dq_ref[t] = jnp.concatenate(rows, axis=0).astype(BF16)
    for j in range(1, 8):
        send_back(j).wait_send()
    out_k.wait()
    out_v.wait()


def local(queries, attn_out, grad_out, log_norms, query_starts, keys, values):
    scaling = queries.shape[-1] ** (-0.5)
    key_count = keys.shape[0]
    anywhere = pl.BlockSpec(memory_space=pl.ANY)
    sems = [7, 8, 8, len(MOVES), len(MOVES), 16, 16, 16, 16, 8, 8]
    dq, dk, dv = pl.pallas_call(
        functools.partial(kernel, scaling),
        out_shape=(
            jax.ShapeDtypeStruct((2, 64, 128), BF16),
            jax.ShapeDtypeStruct((key_count, 128), BF16),
            jax.ShapeDtypeStruct((key_count, 128), BF16),
        ),
        in_specs=[anywhere] * 7,
        out_specs=(pl.BlockSpec(memory_space=pltpu.VMEM), anywhere, anywhere),
        scratch_shapes=[
            pltpu.VMEM((2, 64, 128), BF16),
            pltpu.VMEM((2, 64, 128), BF16),
            pltpu.VMEM((2, 64, 128), BF16),
            pltpu.VMEM((2, 64), F32),
            pltpu.SMEM((512,), jnp.int32),
            pltpu.VMEM((key_count, 128), BF16),
            pltpu.VMEM((key_count, 128), BF16),
            pltpu.VMEM((128, key_count), BF16),
            pltpu.VMEM((key_count, 128), F32),
            pltpu.VMEM((8, 48, 128), BF16),
            pltpu.VMEM((8, 48, 128), BF16),
            pltpu.VMEM((32, BLOCK, 128), BF16),
            pltpu.VMEM((32, 128, ROWS), F32),
            pltpu.VMEM((32, 128, ROWS), BF16),
            pltpu.VMEM((16, 128, ROWS), BF16),
            pltpu.VMEM((16, 128, ROWS), BF16),
            pltpu.VMEM((16, 128, ROWS), BF16),
            pltpu.VMEM((16, key_count, 2 * ROWS), BF16),
            pltpu.VMEM((16, key_count, 2 * ROWS), BF16),
            pltpu.VMEM((key_count, 128), BF16),
            pltpu.VMEM((key_count, 128), BF16),
            pltpu.VMEM((ROWS, 128), BF16),
            pltpu.VMEM((8, 16, 128), BF16),
            *[pltpu.SemaphoreType.DMA((n,)) for n in sems],
        ],
        cost_estimate=pl.CostEstimate(
            flops=10 * 4096 * key_count * 128,
            bytes_accessed=4 * key_count * 256,
            transcendentals=4096 * key_count,
        ),
        compiler_params=pltpu.CompilerParams(
            collective_id=0, has_side_effects=True, vmem_limit_bytes=60 * 1024 * 1024
        ),
    )(
        queries, attn_out, grad_out, log_norms, query_starts,
        keys.reshape(key_count, 128), values.reshape(key_count, 128),
    )
    return dq, dk[:, None, :], dv[:, None, :]


def solution(mesh):
    return jax.shard_map(
        local,
        mesh=mesh,
        in_specs=(
            P(("seq", "kvh"), None, None),
            P(("seq", "kvh"), None, None),
            P(("seq", "kvh"), None, None),
            P(("seq", "kvh"), None),
            P(),
            P("seq", "kvh", None),
            P("seq", "kvh", None),
        ),
        out_specs=(P(("seq", "kvh"), None, None), P("seq", "kvh", None), P("seq", "kvh", None)),
        check_vma=False,
    )
```

```python
import functools
import math

import jax
import jax.numpy as jnp
from jax import lax
from jax.experimental import pallas as pl
from jax.experimental.pallas import tpu as pltpu
from jax.sharding import PartitionSpec as P

F32, BF16 = jnp.float32, jnp.bfloat16
MESH = pl.DeviceIdType.MESH

ROWS = 128
BLOCK = 2 * ROWS + 16
CHUNKS = (
    (("o", (0, 0)), ("s", (0, 0))),
    (("o", (1, 0)), ("o", (3, 0))),
    (("s", (1, 0)), ("s", (3, 0))),
    (("o", (2, 0)), ("s", (2, 0))),
    (("o", (1, 1)), ("o", (1, 3))),
    (("o", (3, 1)), ("o", (3, 3))),
    (("s", (1, 1)), ("s", (1, 3))),
    (("s", (3, 1)), ("s", (3, 3))),
    (("o", (1, 2)), ("o", (3, 2))),
    (("o", (2, 2)), ("s", (2, 2))),
    (("s", (1, 2)), ("s", (3, 2))),
    (("o", (2, 1)), ("o", (2, 3))),
    (("s", (2, 1)), ("s", (2, 3))),
    (("o", (0, 2)), ("s", (0, 2))),
    (("o", (0, 1)), ("o", (0, 3))),
    (("s", (0, 1)), ("s", (0, 3))),
)
ARRIVE = {
    1: ((1, 0), (3, 0)),
    2: ((2, 0),),
    4: ((1, 1), (1, 3)),
    5: ((3, 1), (3, 3)),
    8: ((1, 2), (3, 2), (2, 2)),
    10: ((2, 1), (2, 3)),
    12: ((0, 2),),
    13: ((0, 1), (0, 3)),
}
LATE_AT = 2
LATE = ((0, 2), (0, 1), (0, 3))
LAG = 3
SLOT = {name: 2 * c + i for c, pair in enumerate(CHUNKS) for i, name in enumerate(pair)}
CHUNK_OF = {name: c for c, pair in enumerate(CHUNKS) for name in pair}
PLACES = [(a, b) for a in range(4) for b in range(4)]
NUMBER = {place: i for i, place in enumerate(PLACES)}
MOVES = []
for _d in [(2, 0), (1, 0), (3, 0), (1, 1), (1, 3), (3, 1), (3, 3), (0, 2), (0, 1), (0, 3)]:
    MOVES += [((0, 0), _d, _d)]
for _s, _d in [((1, 0), (1, 2)), ((3, 0), (3, 2)), ((2, 0), (2, 2)), ((2, 0), (2, 1)), ((2, 0), (2, 3))]:
    MOVES += [(_s, _d, (0, _d[1]))]
MOVES = [(place, place, "sib") for place in PLACES] + MOVES


def kernel(
    scaling,
    q_hbm, o_hbm, g_hbm, n_hbm, st_hbm, k_hbm, v_hbm,
    dq_ref, dk_half, dv_half,
    q_in, o_in, g_in, n_in, st_in, keys, vals, keys_t, jpos,
    stage, landed, blocks, part, part_half, part_in, total_half, total_in,
    score_buf, weight_buf, fin, fin_in,
    in_sem, az_send, az_recv, mv_send, mv_recv, ps_send, ps_recv, tt_send, tt_recv,
    fz_send, fz_recv,
):
    s, k = lax.axis_index("seq"), lax.axis_index("kvh")
    x, y, core = s // 8, (s // 2) % 4, s % 2
    pa, pb = (1 - core) * x + core * y, (1 - core) * y + core * x

    def at(a, b):
        return (1 - core) * ((a * 4 + b) * 2) + core * ((b * 4 + a) * 2 + 1)

    sibling = s + 1 - 2 * core
    target = {
        "sib": sibling,
    }
    for a, b in PLACES[1:]:
        target[a, b] = at((pa + a) % 4, (pb + b) % 4)

    ins = [
        pltpu.make_async_copy(src, dst, in_sem.at[i])
        for i, (src, dst) in enumerate(
            (
                (g_hbm, g_in), (o_hbm, o_in), (n_hbm, n_in), (st_hbm, st_in), (q_hbm, q_in),
                (k_hbm, keys), (v_hbm, vals),
            )
        )
    ]
    for copy in ins:
        copy.start()

    barrier = pltpu.get_barrier_semaphore()
    for j in range(1, 8):
        pl.semaphore_signal(
            barrier, inc=1, device_id={"kvh": (k + j) % 8}, device_id_type=MESH
        )
    for a, b in PLACES[1:]:
        pl.semaphore_signal(
            barrier, inc=1, device_id={"seq": at((pa + a) % 4, (pb + b) % 4)}, device_id_type=MESH
        )
    pl.semaphore_signal(barrier, inc=1, device_id={"seq": sibling}, device_id_type=MESH)

    def move(n):
        source, dest, way = MOVES[n]
        kind = "s" if way == "sib" else "o"
        return pltpu.make_async_remote_copy(
            src_ref=blocks.at[SLOT["o", source]],
            dst_ref=blocks.at[SLOT[kind, dest]],
            send_sem=mv_send.at[n],
            recv_sem=mv_recv.at[n],
            device_id={"seq": target[way]},
            device_id_type=MESH,
        )

    def pass_on(place):
        for n, m in enumerate(MOVES):
            if m[0] == place and (m[1] not in LATE or m[2] == "sib"):
                move(n).start()

    def pass_late():
        for n, m in enumerate(MOVES):
            if m[0] == (0, 0) and m[1] in LATE:
                move(n).start()

    def arrived(kind, place):
        for n, m in enumerate(MOVES):
            if m[1] == place and (m[2] == "sib") == (kind == "s"):
                move(n).wait_recv()

    def give_part(place):
        n = NUMBER[place]
        return pltpu.make_async_remote_copy(
            src_ref=part_half.at[SLOT["s", place]],
            dst_ref=part_in.at[n],
            send_sem=ps_send.at[n],
            recv_sem=ps_recv.at[n],
            device_id={"seq": sibling},
            device_id_type=MESH,
        )

    def give_total(place):
        n = NUMBER[place]
        a, b = place
        return pltpu.make_async_remote_copy(
            src_ref=total_half.at[n],
            dst_ref=total_in.at[n],
            send_sem=tt_send.at[n],
            recv_sem=tt_recv.at[n],
            device_id={"seq": at((pa - a + 4) % 4, (pb - b + 4) % 4)},
            device_id_type=MESH,
        )

    def combine(place):
        give_part(place).wait_recv()
        n = NUMBER[place]
        both = part[SLOT["o", place]] + part_in[n].astype(F32)
        if place == (0, 0):
            part[SLOT["o", place]] = both
        else:
            total_half[n] = both.astype(BF16)
            give_total(place).start()

    for copy in ins[:5]:
        copy.wait()
    heads = 8
    grads = g_in[...].astype(F32)
    queries = q_in[...].astype(F32)
    for j in range(8):
        rows = slice(heads * j, heads * (j + 1))
        stage[j, 0:16] = jnp.concatenate([queries[0, rows], queries[1, rows]], axis=0).astype(BF16)
        stage[j, 16:32] = jnp.concatenate([grads[0, rows], grads[1, rows]], axis=0).astype(BF16)
    product = (grads * o_in[...].astype(F32)).reshape(ROWS, 128)
    product_hi = product.astype(BF16)
    product_lo = (product - product_hi.astype(F32)).astype(BF16)
    ones = jnp.ones((16, 128), BF16)
    contract_last = (((1,), (1,)), ((), ()))
    delta = lax.dot_general(ones, product_hi, contract_last, preferred_element_type=F32)
    delta = delta + lax.dot_general(ones, product_lo, contract_last, preferred_element_type=F32)
    norm = n_in[...] * math.log2(math.e)
    norm = jnp.broadcast_to(
        jnp.concatenate([norm[0:1], norm[1:2]], axis=1), (16, 128)
    )

    row = lax.broadcasted_iota(jnp.int32, (16, 128), 0)
    lane = lax.broadcasted_iota(jnp.int32, (16, 128), 1)
    token = 16 * s + 2 * k
    start = jnp.where(lane < 64, st_in[token], st_in[token + 1])

    def parts_of(value):
        hi = value.astype(BF16).astype(F32)
        mid = (value - hi).astype(BF16).astype(F32)
        return hi, mid, value - hi - mid

    numbers = (
        *parts_of(norm),
        *parts_of(delta),
        (start // 128).astype(F32),
        (start % 128).astype(F32),
        jnp.full((16, 128), s, jnp.int32).astype(F32),
    )
    base = jnp.zeros((16, 128), F32)
    for i, value in enumerate(numbers):
        base = jnp.where(row == i, value, base)
    big_row = lax.broadcasted_iota(jnp.int32, (128, 128), 0)
    big_lane = lax.broadcasted_iota(jnp.int32, (128, 128), 1)
    spread = jnp.concatenate([base] * 8, axis=0)
    spread = jnp.where((big_lane % 64) // 8 == big_row // 16, spread, 0.0).astype(BF16)
    places = 16 * k + 8 * (big_row // 64) + big_row % 8
    pick = jnp.where(big_lane == places, 1.0, 0.0).astype(BF16)
    spread = jnp.dot(spread, pick, preferred_element_type=F32).astype(BF16)
    for j in range(8):
        stage[j, 32:48] = spread[16 * j : 16 * (j + 1)]

    pl.semaphore_wait(barrier, 7 + 15 + 1)

    def hand_out(j):
        peer = (k + j) % 8
        return pltpu.make_async_remote_copy(
            src_ref=stage.at[peer],
            dst_ref=landed.at[k],
            send_sem=az_send.at[j],
            recv_sem=az_recv.at[j],
            device_id={"kvh": peer},
            device_id_type=MESH,
        )

    def hand_in(j):
        return pltpu.make_async_remote_copy(
            src_ref=stage.at[(k + j) % 8],
            dst_ref=landed.at[(k + 8 - j) % 8],
            send_sem=az_send.at[j],
            recv_sem=az_recv.at[j],
            device_id={"kvh": (k + j) % 8},
            device_id_type=MESH,
        )

    for j in (4, 3, 5, 2, 6, 1, 7):
        hand_out(j).start()
    landed[k] = stage[k]
    key_count = keys.shape[0]
    for copy in ins[5:]:
        copy.wait()
    keys_t[...] = keys[...].astype(F32).T.astype(BF16)
    is_last = jnp.where(s == 31, 1.0, 0.0).astype(F32)
    sign = 1.0 - 2.0 * is_last
    jpos[...] = sign * lax.broadcasted_iota(jnp.int32, (key_count, 128), 0).astype(F32)
    for j in range(1, 8):
        hand_in(j).wait_recv()
    mine = SLOT["o", (0, 0)]
    aux = jnp.zeros((16, 128), F32)
    for j in range(8):
        blocks[mine, 16 * j : 16 * (j + 1)] = landed[j, 0:16]
        blocks[mine, ROWS + 16 * j : ROWS + 16 * (j + 1)] = landed[j, 16:32]
        aux = aux + landed[j, 32:48].astype(F32)
    blocks[mine, 2 * ROWS : BLOCK] = aux.astype(BF16)
    pass_on((0, 0))

    shift = (s * key_count).astype(F32)
    in_block = (lax.broadcasted_iota(jnp.int32, (1, 256), 1) % 128) // 8
    last_bound = -(512.0 + in_block.astype(F32))
    factor = scaling * math.log2(math.e)
    tile = 256

    def rows_of(c, first):
        return blocks[pl.ds(2 * c, 2), first : first + ROWS].reshape(2 * ROWS, 128)

    def query_part(c):
        dq = jnp.dot(keys_t[...], score_buf[c], preferred_element_type=F32)
        for i in range(2):
            mine = dq[:, i * ROWS : (i + 1) * ROWS]
            part[2 * c + i] = mine
            part_half[2 * c + i] = mine.astype(BF16)

    def events(at_chunk):
        for place in ARRIVE.get(at_chunk, ()):
            arrived("o", place)
            pass_on(place)
        if at_chunk == LATE_AT:
            pass_late()
        for kind, place in CHUNKS[at_chunk]:
            if kind == "s":
                arrived("s", place)
        for place in PLACES:
            if CHUNK_OF["s", place] + LAG == at_chunk:
                combine(place)

    def give(at_chunk):
        if at_chunk:
            for kind, place in CHUNKS[at_chunk - 1]:
                if kind == "s":
                    give_part(place).start()

    def by_chunk(c, low, high, do):
        if high - low == 1:
            do(low)
            return
        middle = (low + high) // 2

        def lower():
            by_chunk(c, low, middle, do)

        def upper():
            by_chunk(c, middle, high, do)

        lax.cond(c < middle, lower, upper)

    def chunk_step(c, carry):
        by_chunk(c, 0, 16, events)

        before = jnp.maximum(c - 1, 0)
        query_part(before)
        aux = jnp.concatenate(
            [blocks[2 * c + i, 2 * ROWS : BLOCK].astype(F32) for i in range(2)], axis=1
        )
        norm = aux[0:1] + aux[1:2] + aux[2:3]
        delta = aux[3:4] + aux[4:5] + aux[5:6]
        first = aux[6:7] * 128.0 + aux[7:8] - shift
        bound = jnp.where(is_last > 0.5, last_bound - 16.0 * aux[8:9], first)
        q, g = rows_of(c, 0), rows_of(c, ROWS)
        for t in range(key_count // tile):
            here = slice(t * tile, (t + 1) * tile)
            scores = lax.dot_general(keys[here], q, contract_last, preferred_element_type=F32)
            pos = jpos[here]
            pos = jnp.concatenate([pos, pos], axis=1)
            weights = jnp.where(pos >= bound, jnp.exp2(scores * factor - norm), 0.0)
            grads = lax.dot_general(vals[here], g, contract_last, preferred_element_type=F32)
            weight_buf[c, here] = weights.astype(BF16)
            score_buf[c, here] = (weights * (grads - delta)).astype(BF16)

        by_chunk(c, 0, 16, give)
        return carry

    score_buf[0] = jnp.zeros(score_buf.shape[1:], BF16)
    lax.fori_loop(0, 16, chunk_step, 0)
    query_part(15)
    for kind, place in CHUNKS[15]:
        if kind == "s":
            give_part(place).start()

    late = [place for place in PLACES if CHUNK_OF["s", place] + LAG > 15]
    late = sorted(late, key=lambda place: CHUNK_OF["s", place])
    final = [place for place in late if CHUNK_OF["s", place] >= 14]
    for place in late:
        if place not in final:
            combine(place)

    def key_tile(t, carry):
        def middle():
            for place in final:
                combine(place)

        if isinstance(t, int):
            here = slice(t * tile, (t + 1) * tile)
        else:
            pl.when(t == 1)(middle)
            here = pl.ds(pl.multiple_of(t * tile, tile), tile)
        dk = jnp.zeros((tile, 128), F32)
        dv = jnp.zeros((tile, 128), F32)
        for c in range(16):
            dk = dk + jnp.dot(score_buf[c, here], rows_of(c, 0), preferred_element_type=F32)
            dv = dv + jnp.dot(weight_buf[c, here], rows_of(c, ROWS), preferred_element_type=F32)
        dk_half[here] = (dk * scaling).astype(BF16)
        dv_half[here] = dv.astype(BF16)
        return carry

    tiles = key_count // tile
    lax.fori_loop(0, tiles - 1, key_tile, 0)

    total = part[SLOT["o", (0, 0)]]
    for place in PLACES[1:]:
        give_total(place).wait_recv()
        total = total + total_in[NUMBER[place]].astype(F32)
    fin[...] = (total.T * scaling).astype(BF16)

    def send_back(j):
        peer = (k + j) % 8
        return pltpu.make_async_remote_copy(
            src_ref=fin.at[pl.ds(pl.multiple_of(16 * peer, 16), 16)],
            dst_ref=fin_in.at[k],
            send_sem=fz_send.at[j],
            recv_sem=fz_recv.at[j],
            device_id={"kvh": peer},
            device_id_type=MESH,
        )

    def come_back(j):
        peer = (k + j) % 8
        return pltpu.make_async_remote_copy(
            src_ref=fin.at[pl.ds(pl.multiple_of(16 * peer, 16), 16)],
            dst_ref=fin_in.at[(k + 8 - j) % 8],
            send_sem=fz_send.at[j],
            recv_sem=fz_recv.at[j],
            device_id={"kvh": peer},
            device_id_type=MESH,
        )

    for j in (4, 3, 5, 2, 6, 1, 7):
        send_back(j).start()
    key_tile(tiles - 1, 0)
    fin_in[k] = fin[pl.ds(pl.multiple_of(16 * k, 16), 16)]

    for n in range(len(MOVES)):
        move(n).wait_send()
    for place in PLACES:
        give_part(place).wait_send()
        if place != (0, 0):
            give_total(place).wait_send()
    for j in range(1, 8):
        hand_out(j).wait_send()
    for j in range(1, 8):
        come_back(j).wait_recv()
    both = [fin_in[j].astype(F32) for j in range(8)]
    for t in range(2):
        rows = [b[8 * t : 8 * (t + 1)] for b in both]
        dq_ref[t] = jnp.concatenate(rows, axis=0).astype(BF16)
    for j in range(1, 8):
        send_back(j).wait_send()


def write_out(dq_in, dk_in, dv_in, dq_ref, dk_ref, dv_ref, sem):
    copies = [
        pltpu.make_async_copy(src, dst, sem.at[i])
        for i, (src, dst) in enumerate(((dk_in, dk_ref), (dv_in, dv_ref), (dq_in, dq_ref)))
    ]
    for copy in copies:
        copy.start()
    for copy in copies:
        copy.wait()


def local(queries, attn_out, grad_out, log_norms, query_starts, keys, values):
    scaling = queries.shape[-1] ** (-0.5)
    key_count = keys.shape[0]
    anywhere = pl.BlockSpec(memory_space=pl.ANY)
    in_hbm = pl.BlockSpec(memory_space=pltpu.HBM)
    sems = [7, 8, 8, len(MOVES), len(MOVES), 16, 16, 16, 16, 8, 8]
    dq, dk, dv = pl.pallas_call(
        functools.partial(kernel, scaling),
        out_shape=(
            pltpu.VMEM((2, 64, 128), BF16),
            pltpu.VMEM((key_count, 128), BF16),
            pltpu.VMEM((key_count, 128), BF16),
        ),
        in_specs=[in_hbm] * 7,
        out_specs=(pl.BlockSpec(memory_space=pltpu.VMEM),) * 3,
        scratch_shapes=[
            pltpu.VMEM((2, 64, 128), BF16),
            pltpu.VMEM((2, 64, 128), BF16),
            pltpu.VMEM((2, 64, 128), BF16),
            pltpu.VMEM((2, 64), F32),
            pltpu.SMEM((512,), jnp.int32),
            pltpu.VMEM((key_count, 128), BF16),
            pltpu.VMEM((key_count, 128), BF16),
            pltpu.VMEM((128, key_count), BF16),
            pltpu.VMEM((key_count, 128), F32),
            pltpu.VMEM((8, 48, 128), BF16),
            pltpu.VMEM((8, 48, 128), BF16),
            pltpu.VMEM((32, BLOCK, 128), BF16),
            pltpu.VMEM((32, 128, ROWS), F32),
            pltpu.VMEM((32, 128, ROWS), BF16),
            pltpu.VMEM((16, 128, ROWS), BF16),
            pltpu.VMEM((16, 128, ROWS), BF16),
            pltpu.VMEM((16, 128, ROWS), BF16),
            pltpu.VMEM((16, key_count, 2 * ROWS), BF16),
            pltpu.VMEM((16, key_count, 2 * ROWS), BF16),
            pltpu.VMEM((ROWS, 128), BF16),
            pltpu.VMEM((8, 16, 128), BF16),
            *[pltpu.SemaphoreType.DMA((n,)) for n in sems],
        ],
        cost_estimate=pl.CostEstimate(
            flops=10 * 4096 * key_count * 128,
            bytes_accessed=4 * key_count * 256,
            transcendentals=4096 * key_count,
        ),
        compiler_params=pltpu.CompilerParams(
            collective_id=0, has_side_effects=True, vmem_limit_bytes=59 * 1024 * 1024
        ),
    )(
        queries, attn_out, grad_out, log_norms, query_starts,
        keys.reshape(key_count, 128), values.reshape(key_count, 128),
    )
    dq, dk, dv = pl.pallas_call(
        write_out,
        out_shape=(
            jax.ShapeDtypeStruct((2, 64, 128), BF16),
            jax.ShapeDtypeStruct((key_count, 128), BF16),
            jax.ShapeDtypeStruct((key_count, 128), BF16),
        ),
        in_specs=[pl.BlockSpec(memory_space=pltpu.VMEM)] * 3,
        out_specs=(anywhere,) * 3,
        scratch_shapes=[pltpu.SemaphoreType.DMA((3,))],
        compiler_params=pltpu.CompilerParams(vmem_limit_bytes=1024 * 1024),
    )(dq, dk, dv)
    return dq, dk[:, None, :], dv[:, None, :]


def solution(mesh):
    return jax.shard_map(
        local,
        mesh=mesh,
        in_specs=(
            P(("seq", "kvh"), None, None),
            P(("seq", "kvh"), None, None),
            P(("seq", "kvh"), None, None),
            P(("seq", "kvh"), None),
            P(),
            P("seq", "kvh", None),
            P("seq", "kvh", None),
        ),
        out_specs=(P(("seq", "kvh"), None, None), P("seq", "kvh", None), P("seq", "kvh", None)),
        check_vma=False,
    )
```

```python
import functools
import math

import jax
import jax.numpy as jnp
from jax import lax
from jax.experimental import pallas as pl
from jax.experimental.pallas import tpu as pltpu
from jax.sharding import PartitionSpec as P

F32, BF16 = jnp.float32, jnp.bfloat16
MESH = pl.DeviceIdType.MESH

ROWS = 128
BLOCK = 2 * ROWS + 16
CHUNKS = (
    ((1, 0), (3, 0)),
    ((0, 0), (2, 0)),
    ((1, 1), (1, 3)),
    ((1, 2), (3, 2)),
    ((2, 2), (2, 1)),
    ((2, 3), (0, 2)),
    ((3, 1), (3, 3)),
    ((0, 1), (0, 3)),
)
N_CHUNKS = len(CHUNKS)
ARRIVE = {
    0: ((1, 0), (3, 0)),
    2: ((1, 1), (1, 3)),
    3: ((1, 2), (3, 2)),
    4: ((2, 2), (2, 1)),
    5: ((2, 3), (0, 2)),
    6: ((3, 1), (3, 3)),
    7: ((0, 1), (0, 3)),
}
BETWEEN = {0: ((2, 0),)}
LATE_AT = 2
LATE = ((0, 2), (0, 1), (0, 3))
SLOT = {place: 2 * c + i for c, pair in enumerate(CHUNKS) for i, place in enumerate(pair)}
PLACES = [(a, b) for a in range(4) for b in range(4)]
MOVES = []
for _d in [(2, 0), (1, 0), (3, 0), (1, 1), (1, 3), (3, 1), (3, 3), (0, 2), (0, 1), (0, 3)]:
    MOVES += [((0, 0), _d, _d)]
for _s, _d in [((1, 0), (1, 2)), ((3, 0), (3, 2)), ((2, 0), (2, 2)), ((2, 0), (2, 1)), ((2, 0), (2, 3))]:
    MOVES += [(_s, _d, (0, _d[1]))]


def kernel(
    scaling,
    q_hbm, o_hbm, g_hbm, n_hbm, st_hbm, k_hbm, v_hbm,
    dq_ref, dk_half, dv_half,
    q_in, o_in, g_in, n_in, st_in, keys, vals, keys_t, jpos,
    stage, landed, blocks, part, total_half, total_in,
    score_buf, weight_buf, other_k, other_v, own_k, own_v, got_k, got_v, fin, fin_in,
    in_sem, az_send, az_recv, mv_send, mv_recv, xs_send, xs_recv, tt_send, tt_recv,
    fz_send, fz_recv,
):
    s, k = lax.axis_index("seq"), lax.axis_index("kvh")
    x, y, core = s // 8, (s // 2) % 4, s % 2
    pa, pb = (1 - core) * x + core * y, (1 - core) * y + core * x

    def at(a, b):
        return (1 - core) * ((a * 4 + b) * 2) + core * ((b * 4 + a) * 2 + 1)

    sibling = s + 1 - 2 * core
    target = {(a, b): at((pa + a) % 4, (pb + b) % 4) for a, b in PLACES[1:]}
    key_count = keys.shape[0] // 2
    mine_at = pl.ds(pl.multiple_of(core * key_count, key_count), key_count)

    ins = [
        pltpu.make_async_copy(src, dst, in_sem.at[i])
        for i, (src, dst) in enumerate(
            (
                (g_hbm, g_in), (o_hbm, o_in), (n_hbm, n_in), (st_hbm, st_in), (q_hbm, q_in),
                (k_hbm, keys.at[mine_at]), (v_hbm, vals.at[mine_at]),
            )
        )
    ]
    for copy in ins:
        copy.start()

    barrier = pltpu.get_barrier_semaphore()
    for j in range(1, 8):
        pl.semaphore_signal(
            barrier, inc=1, device_id={"kvh": (k + j) % 8}, device_id_type=MESH
        )
    for a, b in PLACES[1:]:
        pl.semaphore_signal(
            barrier, inc=1, device_id={"seq": at((pa + a) % 4, (pb + b) % 4)}, device_id_type=MESH
        )
    pl.semaphore_signal(barrier, inc=1, device_id={"seq": sibling}, device_id_type=MESH)

    def move(n):
        source, dest, way = MOVES[n]
        return pltpu.make_async_remote_copy(
            src_ref=blocks.at[SLOT[source]],
            dst_ref=blocks.at[SLOT[dest]],
            send_sem=mv_send.at[n],
            recv_sem=mv_recv.at[n],
            device_id={"seq": target[way]},
            device_id_type=MESH,
        )

    def pass_on(place):
        for n, m in enumerate(MOVES):
            if m[0] == place and m[1] not in LATE:
                move(n).start()

    def pass_late():
        for n, m in enumerate(MOVES):
            if m[0] == (0, 0) and m[1] in LATE:
                move(n).start()

    def arrived(place):
        for n, m in enumerate(MOVES):
            if m[1] == place:
                move(n).wait_recv()

    def to_sibling(n, src, dst):
        return pltpu.make_async_remote_copy(
            src_ref=src,
            dst_ref=dst,
            send_sem=xs_send.at[n],
            recv_sem=xs_recv.at[n],
            device_id={"seq": sibling},
            device_id_type=MESH,
        )

    other_at = pl.ds(pl.multiple_of((1 - core) * key_count, key_count), key_count)
    cached = [to_sibling(n, ref.at[mine_at], ref.at[mine_at]) for n, ref in enumerate((keys, vals))]
    cached_in = [
        to_sibling(n, ref.at[other_at], ref.at[other_at]) for n, ref in enumerate((keys, vals))
    ]
    halves = [to_sibling(2, other_k, got_k), to_sibling(3, other_v, got_v)]

    def give_total(place):
        n = SLOT[place]
        a, b = place
        return pltpu.make_async_remote_copy(
            src_ref=total_half.at[n],
            dst_ref=total_in.at[n],
            send_sem=tt_send.at[n],
            recv_sem=tt_recv.at[n],
            device_id={"seq": at((pa - a + 4) % 4, (pb - b + 4) % 4)},
            device_id_type=MESH,
        )

    for copy in ins[:5]:
        copy.wait()
    heads = 8
    grads = g_in[...].astype(F32)
    queries = q_in[...].astype(F32)
    for j in range(8):
        rows = slice(heads * j, heads * (j + 1))
        stage[j, 0:16] = jnp.concatenate([queries[0, rows], queries[1, rows]], axis=0).astype(BF16)
        stage[j, 16:32] = jnp.concatenate([grads[0, rows], grads[1, rows]], axis=0).astype(BF16)
    product = (grads * o_in[...].astype(F32)).reshape(ROWS, 128)
    product_hi = product.astype(BF16)
    product_lo = (product - product_hi.astype(F32)).astype(BF16)
    ones = jnp.ones((16, 128), BF16)
    contract_last = (((1,), (1,)), ((), ()))
    delta = lax.dot_general(ones, product_hi, contract_last, preferred_element_type=F32)
    delta = delta + lax.dot_general(ones, product_lo, contract_last, preferred_element_type=F32)
    norm = n_in[...] * math.log2(math.e)
    norm = jnp.broadcast_to(
        jnp.concatenate([norm[0:1], norm[1:2]], axis=1), (16, 128)
    )

    row = lax.broadcasted_iota(jnp.int32, (16, 128), 0)
    lane = lax.broadcasted_iota(jnp.int32, (16, 128), 1)
    token = 16 * s + 2 * k
    start = jnp.where(lane < 64, st_in[token], st_in[token + 1])

    def parts_of(value):
        hi = value.astype(BF16).astype(F32)
        mid = (value - hi).astype(BF16).astype(F32)
        return hi, mid, value - hi - mid

    numbers = (
        *parts_of(norm),
        *parts_of(delta),
        (start // 128).astype(F32),
        (start % 128).astype(F32),
        jnp.full((16, 128), s, jnp.int32).astype(F32),
    )
    base = jnp.zeros((16, 128), F32)
    for i, value in enumerate(numbers):
        base = jnp.where(row == i, value, base)
    big_row = lax.broadcasted_iota(jnp.int32, (128, 128), 0)
    big_lane = lax.broadcasted_iota(jnp.int32, (128, 128), 1)
    spread = jnp.concatenate([base] * 8, axis=0)
    spread = jnp.where((big_lane % 64) // 8 == big_row // 16, spread, 0.0).astype(BF16)
    places = 16 * k + 8 * (big_row // 64) + big_row % 8
    pick = jnp.where(big_lane == places, 1.0, 0.0).astype(BF16)
    spread = jnp.dot(spread, pick, preferred_element_type=F32).astype(BF16)
    for j in range(8):
        stage[j, 32:48] = spread[16 * j : 16 * (j + 1)]

    pl.semaphore_wait(barrier, 7 + 15 + 1)

    def hand_out(j):
        peer = (k + j) % 8
        return pltpu.make_async_remote_copy(
            src_ref=stage.at[peer],
            dst_ref=landed.at[k],
            send_sem=az_send.at[j],
            recv_sem=az_recv.at[j],
            device_id={"kvh": peer},
            device_id_type=MESH,
        )

    def hand_in(j):
        return pltpu.make_async_remote_copy(
            src_ref=stage.at[(k + j) % 8],
            dst_ref=landed.at[(k + 8 - j) % 8],
            send_sem=az_send.at[j],
            recv_sem=az_recv.at[j],
            device_id={"kvh": (k + j) % 8},
            device_id_type=MESH,
        )

    for j in (4, 3, 5, 2, 6, 1, 7):
        hand_out(j).start()
    landed[k] = stage[k]
    for copy in ins[5:]:
        copy.wait()
    for copy in cached:
        copy.start()
    for copy in cached_in:
        copy.wait_recv()
    keys_t[...] = keys[...].astype(F32).T.astype(BF16)
    is_last = jnp.where(s // 2 == 15, 1.0, 0.0).astype(F32)
    sign = 1.0 - 2.0 * is_last
    jpos[...] = sign * lax.broadcasted_iota(jnp.int32, jpos.shape, 0).astype(F32)
    for j in range(1, 8):
        hand_in(j).wait_recv()
    mine = SLOT[0, 0]
    aux = jnp.zeros((16, 128), F32)
    for j in range(8):
        blocks[mine, 16 * j : 16 * (j + 1)] = landed[j, 0:16]
        blocks[mine, ROWS + 16 * j : ROWS + 16 * (j + 1)] = landed[j, 16:32]
        aux = aux + landed[j, 32:48].astype(F32)
    blocks[mine, 2 * ROWS : BLOCK] = aux.astype(BF16)
    pass_on((0, 0))

    shift = ((s // 2) * (2 * key_count)).astype(F32)
    in_block = (lax.broadcasted_iota(jnp.int32, (1, 256), 1) % 128) // 8
    last_bound = -(1536.0 + in_block.astype(F32))
    factor = scaling * math.log2(math.e)
    tile = 256

    def rows_of(c, first):
        return blocks[pl.ds(2 * c, 2), first : first + ROWS].reshape(2 * ROWS, 128)

    def query_part(c):
        dq = jnp.dot(keys_t[...], score_buf[c], preferred_element_type=F32)
        for i in range(2):
            mine = dq[:, i * ROWS : (i + 1) * ROWS]
            part[2 * c + i] = mine
            total_half[2 * c + i] = mine.astype(BF16)

    def events(at_chunk):
        for place in ARRIVE.get(at_chunk, ()):
            arrived(place)
            pass_on(place)
        if at_chunk == LATE_AT:
            pass_late()

    def between(at_chunk):
        give(at_chunk)
        for place in BETWEEN.get(at_chunk, ()):
            arrived(place)
            pass_on(place)
        if at_chunk + 0.5 == LATE_AT:
            pass_late()

    def give(at_chunk):
        for place in CHUNKS[at_chunk - 1] if at_chunk else ():
            if place != (0, 0):
                give_total(place).start()

    def by_chunk(c, low, high, do):
        if high - low == 1:
            do(low)
            return
        middle = (low + high) // 2

        def lower():
            by_chunk(c, low, middle, do)

        def upper():
            by_chunk(c, middle, high, do)

        lax.cond(c < middle, lower, upper)

    def chunk_step(c, carry):
        by_chunk(c, 0, N_CHUNKS, events)

        before = jnp.maximum(c - 1, 0)
        query_part(before)
        aux = jnp.concatenate(
            [blocks[2 * c + i, 2 * ROWS : BLOCK].astype(F32) for i in range(2)], axis=1
        )
        norm = aux[0:1] + aux[1:2] + aux[2:3]
        delta = aux[3:4] + aux[4:5] + aux[5:6]
        first = aux[6:7] * 128.0 + aux[7:8] - shift
        bound = jnp.where(is_last > 0.5, last_bound - 16.0 * aux[8:9], first)
        q, g = rows_of(c, 0), rows_of(c, ROWS)
        steps = 2 * key_count // tile
        for t in range(steps):
            if t == steps // 2:
                by_chunk(c, 0, N_CHUNKS, between)
            here = slice(t * tile, (t + 1) * tile)
            scores = lax.dot_general(keys[here], q, contract_last, preferred_element_type=F32)
            pos = jpos[here]
            pos = jnp.concatenate([pos, pos], axis=1)
            weights = jnp.where(pos >= bound, jnp.exp2(scores * factor - norm), 0.0)
            grads = lax.dot_general(vals[here], g, contract_last, preferred_element_type=F32)
            weight_buf[c, here] = weights.astype(BF16)
            score_buf[c, here] = (weights * (grads - delta)).astype(BF16)

        return carry

    score_buf[0] = jnp.zeros(score_buf.shape[1:], BF16)
    lax.fori_loop(0, N_CHUNKS, chunk_step, 0)
    query_part(N_CHUNKS - 1)
    give(N_CHUNKS)

    def key_tile(first, t, k_ref, v_ref):
        rows = pl.ds(pl.multiple_of(first * key_count + t * tile, tile), tile)
        here = pl.ds(pl.multiple_of(t * tile, tile), tile)
        dk = jnp.zeros((tile, 128), F32)
        dv = jnp.zeros((tile, 128), F32)
        for c in range(N_CHUNKS):
            dk = dk + jnp.dot(score_buf[c, rows], rows_of(c, 0), preferred_element_type=F32)
            dv = dv + jnp.dot(weight_buf[c, rows], rows_of(c, ROWS), preferred_element_type=F32)
        k_ref[here] = dk
        v_ref[here] = dv

    tiles = key_count // tile

    def other_tile(t, carry):
        key_tile(1 - core, t, other_k, other_v)
        return carry

    def own_tile(t, carry):
        key_tile(core, t, own_k, own_v)
        return carry

    lax.fori_loop(0, tiles, other_tile, 0)
    for copy in halves:
        copy.start()

    total = part[SLOT[0, 0]]
    for place in PLACES[1:]:
        give_total(place).wait_recv()
        total = total + total_in[SLOT[place]].astype(F32)
    fin[...] = (total.T * scaling).astype(BF16)

    def send_back(j):
        peer = (k + j) % 8
        return pltpu.make_async_remote_copy(
            src_ref=fin.at[pl.ds(pl.multiple_of(16 * peer, 16), 16)],
            dst_ref=fin_in.at[k],
            send_sem=fz_send.at[j],
            recv_sem=fz_recv.at[j],
            device_id={"kvh": peer},
            device_id_type=MESH,
        )

    def come_back(j):
        peer = (k + j) % 8
        return pltpu.make_async_remote_copy(
            src_ref=fin.at[pl.ds(pl.multiple_of(16 * peer, 16), 16)],
            dst_ref=fin_in.at[(k + 8 - j) % 8],
            send_sem=fz_send.at[j],
            recv_sem=fz_recv.at[j],
            device_id={"kvh": peer},
            device_id_type=MESH,
        )

    for j in (4, 3, 5, 2, 6, 1, 7):
        send_back(j).start()
    lax.fori_loop(0, tiles, own_tile, 0)
    for copy in halves:
        copy.wait_recv()
    dk_half[...] = ((own_k[...] + got_k[...]) * scaling).astype(BF16)
    dv_half[...] = (own_v[...] + got_v[...]).astype(BF16)
    fin_in[k] = fin[pl.ds(pl.multiple_of(16 * k, 16), 16)]

    for n in range(len(MOVES)):
        move(n).wait_send()
    for place in PLACES[1:]:
        give_total(place).wait_send()
    for copy in cached + halves:
        copy.wait_send()
    for j in range(1, 8):
        hand_out(j).wait_send()
    for j in range(1, 8):
        come_back(j).wait_recv()
    both = [fin_in[j].astype(F32) for j in range(8)]
    for t in range(2):
        rows = [b[8 * t : 8 * (t + 1)] for b in both]
        dq_ref[t] = jnp.concatenate(rows, axis=0).astype(BF16)
    for j in range(1, 8):
        send_back(j).wait_send()


def write_out(dq_in, dk_in, dv_in, dq_ref, dk_ref, dv_ref, sem):
    copies = [
        pltpu.make_async_copy(src, dst, sem.at[i])
        for i, (src, dst) in enumerate(((dk_in, dk_ref), (dv_in, dv_ref), (dq_in, dq_ref)))
    ]
    for copy in copies:
        copy.start()
    for copy in copies:
        copy.wait()


def local(queries, attn_out, grad_out, log_norms, query_starts, keys, values):
    scaling = queries.shape[-1] ** (-0.5)
    key_count = keys.shape[0]
    anywhere = pl.BlockSpec(memory_space=pl.ANY)
    in_hbm = pl.BlockSpec(memory_space=pltpu.HBM)
    sems = [7, 8, 8, len(MOVES), len(MOVES), 4, 4, 16, 16, 8, 8]
    dq, dk, dv = pl.pallas_call(
        functools.partial(kernel, scaling),
        out_shape=(
            pltpu.VMEM((2, 64, 128), BF16),
            pltpu.VMEM((key_count, 128), BF16),
            pltpu.VMEM((key_count, 128), BF16),
        ),
        in_specs=[in_hbm] * 7,
        out_specs=(pl.BlockSpec(memory_space=pltpu.VMEM),) * 3,
        scratch_shapes=[
            pltpu.VMEM((2, 64, 128), BF16),
            pltpu.VMEM((2, 64, 128), BF16),
            pltpu.VMEM((2, 64, 128), BF16),
            pltpu.VMEM((2, 64), F32),
            pltpu.SMEM((512,), jnp.int32),
            pltpu.VMEM((2 * key_count, 128), BF16),
            pltpu.VMEM((2 * key_count, 128), BF16),
            pltpu.VMEM((128, 2 * key_count), BF16),
            pltpu.VMEM((2 * key_count, 128), F32),
            pltpu.VMEM((8, 48, 128), BF16),
            pltpu.VMEM((8, 48, 128), BF16),
            pltpu.VMEM((16, BLOCK, 128), BF16),
            pltpu.VMEM((16, 128, ROWS), F32),
            pltpu.VMEM((16, 128, ROWS), BF16),
            pltpu.VMEM((16, 128, ROWS), BF16),
            pltpu.VMEM((N_CHUNKS, 2 * key_count, 2 * ROWS), BF16),
            pltpu.VMEM((N_CHUNKS, 2 * key_count, 2 * ROWS), BF16),
            *[pltpu.VMEM((key_count, 128), F32) for _ in range(6)],
            pltpu.VMEM((ROWS, 128), BF16),
            pltpu.VMEM((8, 16, 128), BF16),
            *[pltpu.SemaphoreType.DMA((n,)) for n in sems],
        ],
        cost_estimate=pl.CostEstimate(
            flops=10 * 4096 * key_count * 128,
            bytes_accessed=4 * key_count * 256,
            transcendentals=4096 * key_count,
        ),
        compiler_params=pltpu.CompilerParams(
            collective_id=0, has_side_effects=True, vmem_limit_bytes=59 * 1024 * 1024
        ),
    )(
        queries, attn_out, grad_out, log_norms, query_starts,
        keys.reshape(key_count, 128), values.reshape(key_count, 128),
    )
    dq, dk, dv = pl.pallas_call(
        write_out,
        out_shape=(
            jax.ShapeDtypeStruct((2, 64, 128), BF16),
            jax.ShapeDtypeStruct((key_count, 128), BF16),
            jax.ShapeDtypeStruct((key_count, 128), BF16),
        ),
        in_specs=[pl.BlockSpec(memory_space=pltpu.VMEM)] * 3,
        out_specs=(anywhere,) * 3,
        scratch_shapes=[pltpu.SemaphoreType.DMA((3,))],
        compiler_params=pltpu.CompilerParams(vmem_limit_bytes=1024 * 1024),
    )(dq, dk, dv)
    return dq, dk[:, None, :], dv[:, None, :]


def solution(mesh):
    return jax.shard_map(
        local,
        mesh=mesh,
        in_specs=(
            P(("seq", "kvh"), None, None),
            P(("seq", "kvh"), None, None),
            P(("seq", "kvh"), None, None),
            P(("seq", "kvh"), None),
            P(),
            P("seq", "kvh", None),
            P("seq", "kvh", None),
        ),
        out_specs=(P(("seq", "kvh"), None, None), P("seq", "kvh", None), P("seq", "kvh", None)),
        check_vma=False,
    )
```

```python
import functools
import math

import jax
import jax.numpy as jnp
from jax import lax
from jax.experimental import pallas as pl
from jax.experimental.pallas import tpu as pltpu
from jax.sharding import PartitionSpec as P

F32, BF16 = jnp.float32, jnp.bfloat16
MESH = pl.DeviceIdType.MESH

ROWS = 128
BLOCK = 2 * ROWS + 16
CHUNKS = (
    ((1, 0), (3, 0)),
    ((0, 0), (2, 0)),
    ((1, 1), (1, 3)),
    ((1, 2), (3, 2)),
    ((2, 2), (2, 1)),
    ((2, 3), (0, 2)),
    ((3, 1), (3, 3)),
    ((0, 1), (0, 3)),
)
N_CHUNKS = len(CHUNKS)
ARRIVE = {
    0: ((1, 0), (3, 0)),
    2: ((1, 1), (1, 3)),
    3: ((1, 2), (3, 2)),
    4: ((2, 2), (2, 1)),
    5: ((2, 3), (0, 2)),
    6: ((3, 1), (3, 3)),
    7: ((0, 1), (0, 3)),
}
BETWEEN = {0: ((2, 0),)}
LATE_AT = 2
LATE = ((0, 2), (0, 1), (0, 3))
SLOT = {place: 2 * c + i for c, pair in enumerate(CHUNKS) for i, place in enumerate(pair)}
PLACES = [(a, b) for a in range(4) for b in range(4)]
MOVES = []
for _d in [(2, 0), (1, 0), (3, 0), (1, 1), (1, 3), (3, 1), (3, 3), (0, 2), (0, 1), (0, 3)]:
    MOVES += [((0, 0), _d, _d)]
for _s, _d in [((1, 0), (1, 2)), ((3, 0), (3, 2)), ((2, 0), (2, 2)), ((2, 0), (2, 1)), ((2, 0), (2, 3))]:
    MOVES += [(_s, _d, (0, _d[1]))]


def kernel(
    scaling,
    q_hbm, o_hbm, g_hbm, n_hbm, st_hbm, k_hbm, v_hbm,
    dq_ref, dk_half, dv_half,
    q_in, o_in, g_in, n_in, st_in, keys, vals, keys_t, jpos,
    stage, landed, blocks, part, total_half, total_in,
    score_buf, weight_buf, other_k, other_v, own_k, own_v, got_k, got_v, fin, fin_in,
    in_sem, az_send, az_recv, mv_send, mv_recv, xs_send, xs_recv, tt_send, tt_recv,
    fz_send, fz_recv,
):
    s, k = lax.axis_index("seq"), lax.axis_index("kvh")
    x, y, core = s // 8, (s // 2) % 4, s % 2
    pa, pb = (1 - core) * x + core * y, (1 - core) * y + core * x

    def at(a, b):
        return (1 - core) * ((a * 4 + b) * 2) + core * ((b * 4 + a) * 2 + 1)

    sibling = s + 1 - 2 * core
    target = {(a, b): at((pa + a) % 4, (pb + b) % 4) for a, b in PLACES[1:]}
    key_count = keys.shape[0] // 2
    mine_at = pl.ds(pl.multiple_of(core * key_count, key_count), key_count)

    ins = [
        pltpu.make_async_copy(src, dst, in_sem.at[i])
        for i, (src, dst) in enumerate(
            (
                (g_hbm, g_in), (o_hbm, o_in), (n_hbm, n_in), (st_hbm, st_in), (q_hbm, q_in),
                (k_hbm, keys.at[mine_at]), (v_hbm, vals.at[mine_at]),
            )
        )
    ]
    for copy in ins:
        copy.start()

    barrier = pltpu.get_barrier_semaphore()
    for j in range(1, 8):
        pl.semaphore_signal(
            barrier, inc=1, device_id={"kvh": (k + j) % 8}, device_id_type=MESH
        )
    for a, b in PLACES[1:]:
        pl.semaphore_signal(
            barrier, inc=1, device_id={"seq": at((pa + a) % 4, (pb + b) % 4)}, device_id_type=MESH
        )
    pl.semaphore_signal(barrier, inc=1, device_id={"seq": sibling}, device_id_type=MESH)

    def move(n):
        source, dest, way = MOVES[n]
        return pltpu.make_async_remote_copy(
            src_ref=blocks.at[SLOT[source]],
            dst_ref=blocks.at[SLOT[dest]],
            send_sem=mv_send.at[n],
            recv_sem=mv_recv.at[n],
            device_id={"seq": target[way]},
            device_id_type=MESH,
        )

    def pass_on(place):
        for n, m in enumerate(MOVES):
            if m[0] == place and m[1] not in LATE:
                move(n).start()

    def pass_late():
        for n, m in enumerate(MOVES):
            if m[0] == (0, 0) and m[1] in LATE:
                move(n).start()

    def arrived(place):
        for n, m in enumerate(MOVES):
            if m[1] == place:
                move(n).wait_recv()

    def to_sibling(n, src, dst):
        return pltpu.make_async_remote_copy(
            src_ref=src,
            dst_ref=dst,
            send_sem=xs_send.at[n],
            recv_sem=xs_recv.at[n],
            device_id={"seq": sibling},
            device_id_type=MESH,
        )

    other_at = pl.ds(pl.multiple_of((1 - core) * key_count, key_count), key_count)
    cached = [to_sibling(n, ref.at[mine_at], ref.at[mine_at]) for n, ref in enumerate((keys, vals))]
    cached_in = [
        to_sibling(n, ref.at[other_at], ref.at[other_at]) for n, ref in enumerate((keys, vals))
    ]
    halves = [to_sibling(2, other_k, got_k), to_sibling(3, other_v, got_v)]

    def give_total(place):
        n = SLOT[place]
        a, b = place
        return pltpu.make_async_remote_copy(
            src_ref=total_half.at[n],
            dst_ref=total_in.at[n],
            send_sem=tt_send.at[n],
            recv_sem=tt_recv.at[n],
            device_id={"seq": at((pa - a + 4) % 4, (pb - b + 4) % 4)},
            device_id_type=MESH,
        )

    for copy in ins[:5]:
        copy.wait()
    heads = 8
    grads = g_in[...].astype(F32)
    queries = q_in[...].astype(F32)
    for j in range(8):
        rows = slice(heads * j, heads * (j + 1))
        stage[j, 0:16] = jnp.concatenate([queries[0, rows], queries[1, rows]], axis=0).astype(BF16)
        stage[j, 16:32] = jnp.concatenate([grads[0, rows], grads[1, rows]], axis=0).astype(BF16)
    product = (grads * o_in[...].astype(F32)).reshape(ROWS, 128)
    product_hi = product.astype(BF16)
    product_lo = (product - product_hi.astype(F32)).astype(BF16)
    ones = jnp.ones((16, 128), BF16)
    contract_last = (((1,), (1,)), ((), ()))
    delta = lax.dot_general(ones, product_hi, contract_last, preferred_element_type=F32)
    delta = delta + lax.dot_general(ones, product_lo, contract_last, preferred_element_type=F32)
    norm = n_in[...] * math.log2(math.e)
    norm = jnp.broadcast_to(
        jnp.concatenate([norm[0:1], norm[1:2]], axis=1), (16, 128)
    )

    row = lax.broadcasted_iota(jnp.int32, (16, 128), 0)
    lane = lax.broadcasted_iota(jnp.int32, (16, 128), 1)
    token = 16 * s + 2 * k
    start = jnp.where(lane < 64, st_in[token], st_in[token + 1])

    def parts_of(value):
        hi = value.astype(BF16).astype(F32)
        mid = (value - hi).astype(BF16).astype(F32)
        return hi, mid, value - hi - mid

    numbers = (
        *parts_of(norm),
        *parts_of(delta),
        (start // 128).astype(F32),
        (start % 128).astype(F32),
        jnp.full((16, 128), s, jnp.int32).astype(F32),
    )
    base = jnp.zeros((16, 128), F32)
    for i, value in enumerate(numbers):
        base = jnp.where(row == i, value, base)
    big_row = lax.broadcasted_iota(jnp.int32, (128, 128), 0)
    big_lane = lax.broadcasted_iota(jnp.int32, (128, 128), 1)
    spread = jnp.concatenate([base] * 8, axis=0)
    spread = jnp.where((big_lane % 64) // 8 == big_row // 16, spread, 0.0).astype(BF16)
    places = 16 * k + 8 * (big_row // 64) + big_row % 8
    pick = jnp.where(big_lane == places, 1.0, 0.0).astype(BF16)
    spread = jnp.dot(spread, pick, preferred_element_type=F32).astype(BF16)
    for j in range(8):
        stage[j, 32:48] = spread[16 * j : 16 * (j + 1)]

    pl.semaphore_wait(barrier, 7 + 15 + 1)

    def hand_out(j):
        peer = (k + j) % 8
        return pltpu.make_async_remote_copy(
            src_ref=stage.at[peer],
            dst_ref=landed.at[k],
            send_sem=az_send.at[j],
            recv_sem=az_recv.at[j],
            device_id={"kvh": peer},
            device_id_type=MESH,
        )

    def hand_in(j):
        return pltpu.make_async_remote_copy(
            src_ref=stage.at[(k + j) % 8],
            dst_ref=landed.at[(k + 8 - j) % 8],
            send_sem=az_send.at[j],
            recv_sem=az_recv.at[j],
            device_id={"kvh": (k + j) % 8},
            device_id_type=MESH,
        )

    for j in (4, 3, 5, 2, 6, 1, 7):
        hand_out(j).start()
    landed[k] = stage[k]
    for copy in ins[5:]:
        copy.wait()
    for copy in cached:
        copy.start()
    for copy in cached_in:
        copy.wait_recv()
    keys_t[...] = keys[...].astype(F32).T.astype(BF16)
    is_last = jnp.where(s // 2 == 15, 1.0, 0.0).astype(F32)
    sign = 1.0 - 2.0 * is_last
    jpos[...] = sign * lax.broadcasted_iota(jnp.int32, jpos.shape, 0).astype(F32)
    for j in range(1, 8):
        hand_in(j).wait_recv()
    mine = SLOT[0, 0]
    aux = jnp.zeros((16, 128), F32)
    for j in range(8):
        blocks[mine, 16 * j : 16 * (j + 1)] = landed[j, 0:16]
        blocks[mine, ROWS + 16 * j : ROWS + 16 * (j + 1)] = landed[j, 16:32]
        aux = aux + landed[j, 32:48].astype(F32)
    blocks[mine, 2 * ROWS : BLOCK] = aux.astype(BF16)
    pass_on((0, 0))

    shift = ((s // 2) * (2 * key_count)).astype(F32)
    in_block = (lax.broadcasted_iota(jnp.int32, (1, 256), 1) % 128) // 8
    last_bound = -(1536.0 + in_block.astype(F32))
    factor = scaling * math.log2(math.e)
    tile = 256

    def rows_of(c, first):
        return blocks[pl.ds(2 * c, 2), first : first + ROWS].reshape(2 * ROWS, 128)

    def query_part(c):
        dq = jnp.dot(keys_t[...], score_buf[c], preferred_element_type=F32)
        for i in range(2):
            mine = dq[:, i * ROWS : (i + 1) * ROWS]
            part[2 * c + i] = mine
            total_half[2 * c + i] = mine.astype(BF16)

    def events(at_chunk):
        for place in ARRIVE.get(at_chunk, ()):
            arrived(place)
            pass_on(place)
        if at_chunk == LATE_AT:
            pass_late()

    def between(at_chunk):
        give(at_chunk)
        for place in BETWEEN.get(at_chunk, ()):
            arrived(place)
            pass_on(place)
        if at_chunk + 0.5 == LATE_AT:
            pass_late()

    def give(at_chunk):
        for place in CHUNKS[at_chunk - 1] if at_chunk else ():
            if place != (0, 0):
                give_total(place).start()

    def by_chunk(c, low, high, do):
        if high - low == 1:
            do(low)
            return
        middle = (low + high) // 2

        def lower():
            by_chunk(c, low, middle, do)

        def upper():
            by_chunk(c, middle, high, do)

        lax.cond(c < middle, lower, upper)

    def chunk_step(c, carry):
        by_chunk(c, 0, N_CHUNKS, events)

        before = jnp.maximum(c - 1, 0)
        query_part(before)
        aux = jnp.concatenate(
            [blocks[2 * c + i, 2 * ROWS : BLOCK].astype(F32) for i in range(2)], axis=1
        )
        norm = aux[0:1] + aux[1:2] + aux[2:3]
        delta = aux[3:4] + aux[4:5] + aux[5:6]
        first = aux[6:7] * 128.0 + aux[7:8] - shift
        bound = jnp.where(is_last > 0.5, last_bound - 16.0 * aux[8:9], first)
        q, g = rows_of(c, 0), rows_of(c, ROWS)
        steps = 2 * key_count // tile
        for t in range(steps):
            if t == steps // 2:
                by_chunk(c, 0, N_CHUNKS, between)
            here = slice(t * tile, (t + 1) * tile)
            scores = lax.dot_general(keys[here], q, contract_last, preferred_element_type=F32)
            pos = jpos[here]
            pos = jnp.concatenate([pos, pos], axis=1)
            weights = jnp.where(pos >= bound, jnp.exp2(scores * factor - norm), 0.0)
            grads = lax.dot_general(vals[here], g, contract_last, preferred_element_type=F32)
            weight_buf[c, here] = weights.astype(BF16)
            score_buf[c, here] = (weights * (grads - delta)).astype(BF16)

        return carry

    score_buf[0] = jnp.zeros(score_buf.shape[1:], BF16)
    lax.fori_loop(0, N_CHUNKS, chunk_step, 0)
    query_part(N_CHUNKS - 1)
    give(N_CHUNKS)

    def key_tile(first, t, k_ref, v_ref):
        rows = pl.ds(pl.multiple_of(first * key_count + t * tile, tile), tile)
        here = pl.ds(pl.multiple_of(t * tile, tile), tile)
        dk = jnp.zeros((tile, 128), F32)
        dv = jnp.zeros((tile, 128), F32)
        for c in range(N_CHUNKS):
            dk = dk + jnp.dot(score_buf[c, rows], rows_of(c, 0), preferred_element_type=F32)
            dv = dv + jnp.dot(weight_buf[c, rows], rows_of(c, ROWS), preferred_element_type=F32)
        k_ref[here] = dk
        v_ref[here] = dv

    tiles = key_count // tile

    def other_tile(t, carry):
        key_tile(1 - core, t, other_k, other_v)
        return carry

    def own_tile(t, carry):
        key_tile(core, t, own_k, own_v)
        return carry

    lax.fori_loop(0, tiles, other_tile, 0)
    for copy in halves:
        copy.start()
    lax.fori_loop(0, 1, own_tile, 0)

    total = part[SLOT[0, 0]]
    for place in PLACES[1:]:
        give_total(place).wait_recv()
        total = total + total_in[SLOT[place]].astype(F32)
    fin[...] = (total.T * scaling).astype(BF16)

    def send_back(j):
        peer = (k + j) % 8
        return pltpu.make_async_remote_copy(
            src_ref=fin.at[pl.ds(pl.multiple_of(16 * peer, 16), 16)],
            dst_ref=fin_in.at[k],
            send_sem=fz_send.at[j],
            recv_sem=fz_recv.at[j],
            device_id={"kvh": peer},
            device_id_type=MESH,
        )

    def come_back(j):
        peer = (k + j) % 8
        return pltpu.make_async_remote_copy(
            src_ref=fin.at[pl.ds(pl.multiple_of(16 * peer, 16), 16)],
            dst_ref=fin_in.at[(k + 8 - j) % 8],
            send_sem=fz_send.at[j],
            recv_sem=fz_recv.at[j],
            device_id={"kvh": peer},
            device_id_type=MESH,
        )

    for j in (4, 3, 5, 2, 6, 1, 7):
        send_back(j).start()
    lax.fori_loop(1, tiles, own_tile, 0)
    for copy in halves:
        copy.wait_recv()
    dk_half[...] = ((own_k[...] + got_k[...]) * scaling).astype(BF16)
    dv_half[...] = (own_v[...] + got_v[...]).astype(BF16)
    fin_in[k] = fin[pl.ds(pl.multiple_of(16 * k, 16), 16)]

    for n in range(len(MOVES)):
        move(n).wait_send()
    for place in PLACES[1:]:
        give_total(place).wait_send()
    for copy in cached + halves:
        copy.wait_send()
    for j in range(1, 8):
        hand_out(j).wait_send()
    for j in range(1, 8):
        come_back(j).wait_recv()
    both = [fin_in[j].astype(F32) for j in range(8)]
    for t in range(2):
        rows = [b[8 * t : 8 * (t + 1)] for b in both]
        dq_ref[t] = jnp.concatenate(rows, axis=0).astype(BF16)
    for j in range(1, 8):
        send_back(j).wait_send()


def write_out(dq_in, dk_in, dv_in, dq_ref, dk_ref, dv_ref, sem):
    copies = [
        pltpu.make_async_copy(src, dst, sem.at[i])
        for i, (src, dst) in enumerate(((dk_in, dk_ref), (dv_in, dv_ref), (dq_in, dq_ref)))
    ]
    for copy in copies:
        copy.start()
    for copy in copies:
        copy.wait()


def local(queries, attn_out, grad_out, log_norms, query_starts, keys, values):
    scaling = queries.shape[-1] ** (-0.5)
    key_count = keys.shape[0]
    anywhere = pl.BlockSpec(memory_space=pl.ANY)
    in_hbm = pl.BlockSpec(memory_space=pltpu.HBM)
    sems = [7, 8, 8, len(MOVES), len(MOVES), 4, 4, 16, 16, 8, 8]
    dq, dk, dv = pl.pallas_call(
        functools.partial(kernel, scaling),
        out_shape=(
            pltpu.VMEM((2, 64, 128), BF16),
            pltpu.VMEM((key_count, 128), BF16),
            pltpu.VMEM((key_count, 128), BF16),
        ),
        in_specs=[in_hbm] * 7,
        out_specs=(pl.BlockSpec(memory_space=pltpu.VMEM),) * 3,
        scratch_shapes=[
            pltpu.VMEM((2, 64, 128), BF16),
            pltpu.VMEM((2, 64, 128), BF16),
            pltpu.VMEM((2, 64, 128), BF16),
            pltpu.VMEM((2, 64), F32),
            pltpu.SMEM((512,), jnp.int32),
            pltpu.VMEM((2 * key_count, 128), BF16),
            pltpu.VMEM((2 * key_count, 128), BF16),
            pltpu.VMEM((128, 2 * key_count), BF16),
            pltpu.VMEM((2 * key_count, 128), F32),
            pltpu.VMEM((8, 48, 128), BF16),
            pltpu.VMEM((8, 48, 128), BF16),
            pltpu.VMEM((16, BLOCK, 128), BF16),
            pltpu.VMEM((16, 128, ROWS), F32),
            pltpu.VMEM((16, 128, ROWS), BF16),
            pltpu.VMEM((16, 128, ROWS), BF16),
            pltpu.VMEM((N_CHUNKS, 2 * key_count, 2 * ROWS), BF16),
            pltpu.VMEM((N_CHUNKS, 2 * key_count, 2 * ROWS), BF16),
            *[pltpu.VMEM((key_count, 128), F32) for _ in range(6)],
            pltpu.VMEM((ROWS, 128), BF16),
            pltpu.VMEM((8, 16, 128), BF16),
            *[pltpu.SemaphoreType.DMA((n,)) for n in sems],
        ],
        cost_estimate=pl.CostEstimate(
            flops=10 * 4096 * key_count * 128,
            bytes_accessed=4 * key_count * 256,
            transcendentals=4096 * key_count,
        ),
        compiler_params=pltpu.CompilerParams(
            collective_id=0, has_side_effects=True, vmem_limit_bytes=59 * 1024 * 1024
        ),
    )(
        queries, attn_out, grad_out, log_norms, query_starts,
        keys.reshape(key_count, 128), values.reshape(key_count, 128),
    )
    dq, dk, dv = pl.pallas_call(
        write_out,
        out_shape=(
            jax.ShapeDtypeStruct((2, 64, 128), BF16),
            jax.ShapeDtypeStruct((key_count, 128), BF16),
            jax.ShapeDtypeStruct((key_count, 128), BF16),
        ),
        in_specs=[pl.BlockSpec(memory_space=pltpu.VMEM)] * 3,
        out_specs=(anywhere,) * 3,
        scratch_shapes=[pltpu.SemaphoreType.DMA((3,))],
        compiler_params=pltpu.CompilerParams(vmem_limit_bytes=1024 * 1024),
    )(dq, dk, dv)
    return dq, dk[:, None, :], dv[:, None, :]


def solution(mesh):
    return jax.shard_map(
        local,
        mesh=mesh,
        in_specs=(
            P(("seq", "kvh"), None, None),
            P(("seq", "kvh"), None, None),
            P(("seq", "kvh"), None, None),
            P(("seq", "kvh"), None),
            P(),
            P("seq", "kvh", None),
            P("seq", "kvh", None),
        ),
        out_specs=(P(("seq", "kvh"), None, None), P("seq", "kvh", None), P("seq", "kvh", None)),
        check_vma=False,
    )
```
